512 devices in a mesh: dp: 32 (over z_lo, x, core), tensor: 16 (over y, z_hi).
Axes of the slice: x: 4, y: 8, z: 8 (z_hi: 2, z_lo: 4; z = z_hi * 4 + z_lo), core: 2. Of those that a mesh axis runs over, the one named last changes fastest.
Arguments:
- tokens: bfloat16 [8192, 3072], P('dp', 'tensor'), may hold values from -6 to 6
- keys: bfloat16 [8192, 4096], P('dp', 'tensor'), may hold values from -4 to 4
- values: bfloat16 [8192, 4096], P('dp', 'tensor'), may hold values from -6 to 6
- cotangent: bfloat16 [8192, 4096], P('dp', 'tensor'), may hold values from -48 to 48
- query_weight: bfloat16 [3072, 4096], P('dp', 'tensor'), may hold values from -0.109375 to 0.109375
Outputs:
- grad_query: float32 [3072, 4096], P('dp', 'tensor')
The draws below stay inside these ranges and needn't reach their ends.
All inputs are finite; a program needn't handle non-finite values.
Results may differ from the reference program's by a relative error of at most 0.04.
Values may be sent and summed in bfloat16 or wider, within the bound.
No kernel may reach another device: no remote copies, remote signals or barrier semaphores. Data moves between devices by JAX's collectives and lax.ppermute only.
A program may use at most 64 MiB of HBM per device.

```python
import math
import jax
import jax.numpy as jnp
from jax import lax

D = 3072
HEAD = 128
IMAGE_TOK = 256
TOK_DEV = 256
HQ = 4096
TOKENS = 8192
N_DP = 32


def with_spikes(drawn, own_key, source, target, parts, factor):
    def block_of(position):
        return (jnp.arange(drawn.shape[position]) // (drawn.shape[position] // parts)).reshape((-1,) + (1,) * (drawn.ndim - 1 - position))

    one_side = jax.random.permutation(own_key, parts)[block_of(target)]
    far = (block_of(target) + parts // 2) % parts
    return jnp.where((block_of(source) == one_side) | (block_of(source) == far), factor * drawn, drawn)


def level_of(rng, dims, shards, least, largest):
    def one(dim, parts):
        heights = jax.random.uniform(jax.random.fold_in(jax.random.fold_in(rng, 6), dim), (parts,), jnp.float32, least / len(shards), largest / len(shards))
        return jnp.repeat(jnp.exp(heights), dims[dim] // parts).reshape((-1,) + (1,) * (len(dims) - dim - 1))

    gain = one(*shards[0])
    for cut in shards[1:]:
        gain = gain * one(*cut)
    return gain


def normal_values(rng, dims, deviation, most, cuts=(), kind=jnp.bfloat16):
    drawn = deviation * jax.random.normal(rng, dims, jnp.float32)
    if cuts:
        drawn = drawn * level_of(rng, dims, cuts, -0.22, 0.18)
    return jnp.clip(drawn, -most, most).astype(kind)


def heavy_noise(stream_key, shape, width, bound, shards, heavy, kind=jnp.bfloat16):
    array = width * jax.random.normal(stream_key, shape, jnp.float32)
    if shards:
        array = array * level_of(stream_key, shape, shards, -0.22, 0.18)
    return jnp.clip(with_spikes(array, jax.random.fold_in(stream_key, 3), *heavy), -bound, bound).astype(kind)


def setup_inputs(seed: int = 0) -> dict:
    seeds = jax.random.split(jax.random.key(seed), 6)
    tokens = heavy_noise(seeds[0], (TOKENS, D), 1.0, 6.0, ((0, 32), (1, 16)), (0, 1, 32, 2.75))
    keys = normal_values(seeds[1], (TOKENS, HQ), 1.0, 4.0, ((0, 32), (1, 16)))
    values = normal_values(seeds[2], (TOKENS, HQ), 1.0, 6.0, ((0, 32), (1, 16)))
    cotangent = normal_values(seeds[3], (TOKENS, HQ), 8.0, 48.0, ((0, 32), (1, 16)))
    query_weight = normal_values(seeds[4], (D, HQ), D ** -0.5, 0.109375, ((0, 32), (1, 16)))
    return {"tokens": tokens, "keys": keys, "values": values, "cotangent": cotangent, "query_weight": query_weight}


def layer_norm(rows):
    rows = rows.astype(jnp.float32)
    center = rows - lax.optimization_barrier(jnp.mean(rows, -1, keepdims=True))
    spread = lax.optimization_barrier(jnp.mean(center * center, -1, keepdims=True))
    return (center * lax.rsqrt(spread + 1e-06)).astype(jnp.bfloat16)

def query_grad(normed, weight, keys, values, cotangent):
    row_count = normed.shape[0]
    col_count = weight.shape[1]
    blocks_shape = (row_count // IMAGE_TOK, IMAGE_TOK, col_count // HEAD, HEAD)
    temper = 1.0 / math.sqrt(HEAD)
    query = jnp.dot(normed, weight, preferred_element_type=jnp.float32).reshape(blocks_shape)
    center = query - lax.optimization_barrier(jnp.mean(query, -1, keepdims=True))
    inverse = lax.rsqrt(lax.optimization_barrier(jnp.mean(center * center, -1, keepdims=True)) + 1e-06)
    normal_query = center * inverse
    key_rows = keys.astype(jnp.float32).reshape(blocks_shape)
    value_rows = values.astype(jnp.float32).reshape(blocks_shape)
    cot_rows = cotangent.astype(jnp.float32).reshape(blocks_shape)
    scores = jnp.einsum('ilhd,imhd->ihlm', normal_query, key_rows) * temper
    expon = jnp.exp(scores)
    attend = expon / lax.optimization_barrier(jnp.sum(expon, -1, keepdims=True))
    pull_prob = jnp.einsum('ilhd,imhd->ihlm', cot_rows, value_rows)
    pull_score = attend * (pull_prob - lax.optimization_barrier(jnp.sum(attend * pull_prob, -1, keepdims=True)))
    pull_normal = jnp.einsum('ihlm,imhd->ilhd', pull_score, key_rows) * temper
    pull_query = inverse * (pull_normal - lax.optimization_barrier(jnp.mean(pull_normal, -1, keepdims=True)) - normal_query * lax.optimization_barrier(jnp.mean(pull_normal * normal_query, -1, keepdims=True)))
    return pull_query.reshape(row_count, col_count).astype(jnp.bfloat16)

def reference(tokens, keys, values, cotangent, query_weight):
    token_scale = 1.0 / jnp.sqrt(jnp.float32(TOKENS))
    normed = layer_norm(tokens)
    col_count = query_weight.shape[1]
    pieces = tuple((a.reshape(N_DP, TOK_DEV, a.shape[1]) for a in (normed, keys, values, cotangent)))

    def summed(weight):

        def accumulate(running, piece):
            normed_rows, key_part, value_part, cot_part = piece
            pull_query = query_grad(normed_rows, weight, key_part, value_part, cot_part)
            term_of = jnp.dot(normed_rows.T, pull_query, preferred_element_type=jnp.float32) * token_scale
            rounded = lax.optimization_barrier(term_of.astype(jnp.bfloat16))
            return (running + rounded.astype(jnp.float32), None)
        running, _ = lax.scan(accumulate, jnp.zeros((D, col_count), jnp.float32), pieces)
        return running
    first = summed(query_weight)
    grad_norm = jnp.sqrt(jnp.sum(first * first))
    factor = 0.3 * jnp.sqrt(jnp.float32(D + col_count)) / grad_norm
    moved = (query_weight.astype(jnp.float32) + factor * first).astype(jnp.bfloat16)
    return summed(moved)
```

```python
import math

import jax
import jax.numpy as jnp
from jax import lax
from jax.experimental import pallas as pl
from jax.experimental.pallas import tpu as pltpu
from jax.sharding import Mesh, PartitionSpec as P

HEAD = 128
ROWS = 96
EPS = 1e-06
F32 = jnp.float32
BF16 = jnp.bfloat16
AXES = ("zl", "x", "core", "y", "zh")
SIZES = (4, 4, 2, 8, 2)
VMEM_LIMIT = 48 * 1024 * 1024


def mm(a, b, dims=((1,), (0,))):
    return lax.dot_general(a, b, (dims, ((), ())), preferred_element_type=F32)


def query_grad(query, keys, values, cotangent):
    temper = 1.0 / math.sqrt(HEAD)
    heads = []
    for h in range(query.shape[1] // HEAD):
        cols = slice(h * HEAD, (h + 1) * HEAD)
        q = query[:, cols]
        key, value, cot = keys[:, cols], values[:, cols], cotangent[:, cols]
        center = q - jnp.mean(q, -1, keepdims=True)
        inverse = lax.rsqrt(jnp.mean(center * center, -1, keepdims=True) + EPS)
        qn = center * inverse
        scores = mm(qn.astype(BF16), key, ((1,), (1,))) * temper
        expon = jnp.exp(scores)
        attend = expon / jnp.sum(expon, -1, keepdims=True)
        dprob = mm(cot, value, ((1,), (1,)))
        dscore = attend * (dprob - jnp.sum(attend * dprob, -1, keepdims=True))
        dqn = mm(dscore.astype(BF16), key) * temper
        dq = inverse * (
            dqn
            - jnp.mean(dqn, -1, keepdims=True)
            - qn * jnp.mean(dqn * qn, -1, keepdims=True)
        )
        heads.append(dq.astype(BF16))
    return jnp.concatenate(heads, axis=1)


def place(y, zh):
    return (2 * (y % 2) + zh) * 4 + y // 2


def first_kernel(scale, at_ref, mine_ref, theirs_ref, w_own_ref, w_oth_ref, keys_ref, values_ref, cot_ref,
                 normt_ref, normed_ref, query_ref, keep_ref, send_ref):
    core, zh = at_ref[0], at_ref[1]
    count = mine_ref.shape[0]
    width = 2 * count * mine_ref.shape[1]
    total = jnp.zeros((1, mine_ref.shape[2]), F32)
    for ref in (mine_ref, theirs_ref):
        for y in range(count):
            total += jnp.sum(ref[y].astype(F32), 0, keepdims=True)
    mean = total / width
    total = jnp.zeros_like(total)
    for ref in (mine_ref, theirs_ref):
        for y in range(count):
            center = ref[y].astype(F32) - mean
            total += jnp.sum(center * center, 0, keepdims=True)
    inverse = lax.rsqrt(total / width + EPS)
    for ref, z in ((mine_ref, zh), (theirs_ref, 1 - zh)):
        for y in range(count):
            block = ((ref[y].astype(F32) - mean) * inverse).astype(BF16)
            for c in range(2):
                half = jnp.bitwise_xor(core, c)
                normt_ref[half, place(y, z)] = block[c * ROWS:(c + 1) * ROWS]
    half_rows = w_own_ref.shape[0]
    for half in range(2):
        rows = normt_ref[half].reshape(half_rows, normt_ref.shape[3])
        normed_ref[:, half * half_rows:(half + 1) * half_rows] = rows.T
    query = mm(normed_ref[:, :half_rows], w_own_ref[...]) + mm(normed_ref[:, half_rows:], w_oth_ref[...])
    query_ref[...] = query
    dq = query_grad(query, keys_ref[...], values_ref[...], cot_ref[...])
    for half, ref in ((0, keep_ref), (1, send_ref)):
        rows = normt_ref[half].reshape(half_rows, normt_ref.shape[3])
        ref[...] = (mm(rows, dq) * scale).astype(BF16).reshape(ref.shape)


def project_kernel(normed_ref, own_ref, oth_ref, out_ref, square_ref):
    half_rows = own_ref.shape[0]
    out_ref[...] = mm(normed_ref[:, :half_rows], own_ref[...]) + mm(normed_ref[:, half_rows:], oth_ref[...])
    own, oth = own_ref[...].astype(F32), oth_ref[...].astype(F32)
    square_ref[...] = jnp.sum((own * own + oth * oth).reshape(-1, 8, own.shape[1]), 0)


def second_kernel(scale, radius, square_ref, query_ref, move_ref, normt_ref, keys_ref, values_ref, cot_ref,
                  keep_ref, send_ref):
    norm = jnp.sqrt(jnp.sum(square_ref[...], keepdims=True))
    query = query_ref[...] + (radius / norm) * move_ref[...]
    dq = query_grad(query, keys_ref[...], values_ref[...], cot_ref[...])
    half_rows = keep_ref.shape[0] * keep_ref.shape[1]
    for half, ref in ((0, keep_ref), (1, send_ref)):
        rows = normt_ref[half].reshape(half_rows, normt_ref.shape[3])
        ref[...] = (mm(rows, dq) * scale).astype(BF16).reshape(ref.shape)


def call(kernel, outs, smem=0):
    spec = pl.BlockSpec(memory_space=pltpu.VMEM)

    def run(*args):
        specs = [pl.BlockSpec(memory_space=pltpu.SMEM)] * smem + [spec] * (len(args) - smem)
        return pl.pallas_call(
            kernel,
            out_shape=[jax.ShapeDtypeStruct(s, d) for s, d in outs],
            in_specs=specs,
            out_specs=[spec] * len(outs),
            compiler_params=pltpu.CompilerParams(vmem_limit_bytes=VMEM_LIMIT),
        )(*args)

    return run


def swap(size, step):
    return [(i, i ^ step) for i in range(size)]


def after(value, *others):
    return lax.optimization_barrier((value, *others))[0]


def gather_dp(shard):
    along_z = lax.all_gather(shard, "zl", axis=0, tiled=True)
    own = lax.all_gather(along_z, "x", axis=0, tiled=True)
    return own, lax.ppermute(own, "core", swap(2, 1))


def scatter_dp(keep, send):
    got = lax.ppermute(send, "core", swap(2, 1))
    both = (keep.astype(F32) + got.astype(F32)).astype(BF16)
    parts = lax.all_to_all(both, ("x", "zl"), 0, 0, tiled=True)
    return jnp.sum(parts.astype(F32), 0)


def shards(tokens, keys, values, cotangent, query_weight):
    tok = tokens.T
    feats, count = tok.shape
    cols = keys.shape[1]
    model_width = feats * 16
    total_tokens = count * 32
    scale = 1.0 / math.sqrt(total_tokens)
    radius = 0.3 * math.sqrt(model_width + cols * 16)
    at = jnp.stack([lax.axis_index("core"), lax.axis_index("zh")]).astype(jnp.int32)

    other = lax.ppermute(tok, "zh", swap(2, 1))
    w_own, w_oth = gather_dp(query_weight)
    mine = lax.all_gather(tok, "y", axis=0)
    other = after(other, mine)
    theirs = lax.all_gather(other, "y", axis=0)

    half = (16, ROWS, cols)
    normt, normed, query, keep, send = call(
        lambda *refs: first_kernel(scale, *refs),
        [((2, 16, ROWS, count), BF16), ((count, model_width), BF16), ((count, cols), F32), (half, BF16), (half, BF16)],
        smem=1,
    )(at, mine, theirs, w_own, w_oth, keys, values, cotangent)

    first = scatter_dp(keep, send)
    own, oth = gather_dp(first.astype(BF16))
    move, square = call(project_kernel, [((count, cols), F32), ((8, cols), F32)])(normed, own, oth)
    square = lax.psum(lax.psum(square, "zh"), "y")
    keep, send = call(
        lambda *refs: second_kernel(scale, radius, *refs), [(half, BF16), (half, BF16)]
    )(square, query, move, normt, keys, values, cotangent)
    return scatter_dp(keep, send)


def solution(mesh):
    cut = Mesh(mesh.devices.reshape(SIZES), AXES)
    spec = P(("zl", "x", "core"), ("y", "zh"))
    return jax.shard_map(shards, mesh=cut, in_specs=(spec,) * 5, out_specs=spec, check_vma=False)
```

```python
import math

import jax
import jax.numpy as jnp
from jax import lax
from jax.experimental import pallas as pl
from jax.experimental.pallas import tpu as pltpu
from jax.sharding import Mesh, PartitionSpec as P

HEAD = 128
ROWS = 96
EPS = 1e-06
F32 = jnp.float32
BF16 = jnp.bfloat16
AXES = ("zl", "x", "core", "y", "zh")
SIZES = (4, 4, 2, 8, 2)
VMEM_LIMIT = 48 * 1024 * 1024


def mm(a, b, dims=((1,), (0,))):
    return lax.dot_general(a, b, (dims, ((), ())), preferred_element_type=F32)


def query_grad(query, keys, values, cotangent):
    temper = 1.0 / math.sqrt(HEAD)
    heads = []
    for h in range(query.shape[1] // HEAD):
        cols = slice(h * HEAD, (h + 1) * HEAD)
        q = query[:, cols]
        key, value, cot = keys[:, cols], values[:, cols], cotangent[:, cols]
        center = q - jnp.mean(q, -1, keepdims=True)
        inverse = lax.rsqrt(jnp.mean(center * center, -1, keepdims=True) + EPS)
        qn = center * inverse
        scores = mm(qn.astype(BF16), key, ((1,), (1,))) * temper
        expon = jnp.exp(scores)
        attend = expon / jnp.sum(expon, -1, keepdims=True)
        dprob = mm(cot, value, ((1,), (1,)))
        dscore = attend * (dprob - jnp.sum(attend * dprob, -1, keepdims=True))
        dqn = mm(dscore.astype(BF16), key) * temper
        dq = inverse * (
            dqn
            - jnp.mean(dqn, -1, keepdims=True)
            - qn * jnp.mean(dqn * qn, -1, keepdims=True)
        )
        heads.append(dq.astype(BF16))
    return jnp.concatenate(heads, axis=1)


def place(y, zh):
    return (2 * (y % 2) + zh) * 4 + y // 2


def first_kernel(scale, at_ref, tok_ref, w_own_ref, w_oth_ref, keys_ref, values_ref, cot_ref,
                 normt_ref, normed_ref, query_ref, keep_ref, send_ref):
    core, zh = at_ref[0], at_ref[1]
    count, width = tok_ref.shape[0], tok_ref.shape[0] * tok_ref.shape[1]
    total = jnp.zeros((1, tok_ref.shape[2]), F32)
    for y in range(count):
        total += jnp.sum(tok_ref[y].astype(F32), 0, keepdims=True)
    mean = total / width
    total = jnp.zeros_like(total)
    for y in range(count):
        center = tok_ref[y].astype(F32) - mean
        total += jnp.sum(center * center, 0, keepdims=True)
    inverse = lax.rsqrt(total / width + EPS)
    for y in range(count):
        block = ((tok_ref[y].astype(F32) - mean) * inverse).astype(BF16)
        for part in range(4):
            half = jnp.bitwise_xor(core, part % 2)
            normt_ref[half, place(y, jnp.bitwise_xor(zh, part // 2))] = block[part * ROWS:(part + 1) * ROWS]
    half_rows = w_own_ref.shape[0]
    for half in range(2):
        rows = normt_ref[half].reshape(half_rows, normt_ref.shape[3])
        normed_ref[:, half * half_rows:(half + 1) * half_rows] = rows.T
    query = mm(normed_ref[:, :half_rows], w_own_ref[...]) + mm(normed_ref[:, half_rows:], w_oth_ref[...])
    query_ref[...] = query
    dq = query_grad(query, keys_ref[...], values_ref[...], cot_ref[...])
    for half, ref in ((0, keep_ref), (1, send_ref)):
        rows = normt_ref[half].reshape(half_rows, normt_ref.shape[3])
        ref[...] = (mm(rows, dq) * scale).astype(BF16).reshape(ref.shape)


def project_kernel(normed_ref, own_ref, oth_ref, out_ref, square_ref):
    half_rows = own_ref.shape[0]
    out_ref[...] = mm(normed_ref[:, :half_rows], own_ref[...]) + mm(normed_ref[:, half_rows:], oth_ref[...])
    own, oth = own_ref[...].astype(F32), oth_ref[...].astype(F32)
    square = jnp.sum((own * own + oth * oth).reshape(-1, 8, own.shape[1]), 0)
    square_ref[...] = square[:, :HEAD] + square[:, HEAD:]


def second_kernel(scale, radius, square_ref, query_ref, move_ref, normt_ref, keys_ref, values_ref, cot_ref,
                  keep_ref, send_ref):
    norm = jnp.sqrt(jnp.sum(jnp.sum(square_ref[...], 0), keepdims=True))
    query = query_ref[...] + (radius / norm) * move_ref[...]
    dq = query_grad(query, keys_ref[...], values_ref[...], cot_ref[...])
    half_rows = keep_ref.shape[0] * keep_ref.shape[1]
    for half, ref in ((0, keep_ref), (1, send_ref)):
        rows = normt_ref[half].reshape(half_rows, normt_ref.shape[3])
        ref[...] = (mm(rows, dq) * scale).astype(BF16).reshape(ref.shape)


def call(kernel, outs, smem=0):
    spec = pl.BlockSpec(memory_space=pltpu.VMEM)

    def run(*args):
        specs = [pl.BlockSpec(memory_space=pltpu.SMEM)] * smem + [spec] * (len(args) - smem)
        return pl.pallas_call(
            kernel,
            out_shape=[jax.ShapeDtypeStruct(s, d) for s, d in outs],
            in_specs=specs,
            out_specs=[spec] * len(outs),
            compiler_params=pltpu.CompilerParams(vmem_limit_bytes=VMEM_LIMIT),
        )(*args)

    return run


def swap(size, step):
    return [(i, i ^ step) for i in range(size)]


def after(value, *others):
    return lax.optimization_barrier((value, *others))[0]


def gather_dp(shard):
    along_z = lax.all_gather(shard, "zl", axis=0, tiled=True)
    own = lax.all_gather(along_z, "x", axis=0, tiled=True)
    return own, lax.ppermute(own, "core", swap(2, 1))


def scatter_dp(keep, send):
    got = lax.ppermute(send, "core", swap(2, 1))
    both = (keep.astype(F32) + got.astype(F32)).astype(BF16)
    parts = lax.all_to_all(both, ("x", "zl"), 0, 0, tiled=True)
    return jnp.sum(parts.astype(F32), 0)


def shards(tokens, keys, values, cotangent, query_weight):
    tok = tokens.T
    feats, count = tok.shape
    cols = keys.shape[1]
    model_width = feats * 16
    total_tokens = count * 32
    scale = 1.0 / math.sqrt(total_tokens)
    radius = 0.3 * math.sqrt(model_width + cols * 16)
    at = jnp.stack([lax.axis_index("core"), lax.axis_index("zh")]).astype(jnp.int32)

    other = lax.ppermute(tok, "zh", swap(2, 1))
    w_own, w_oth = gather_dp(query_weight)
    both = lax.all_gather(jnp.concatenate([tok, other], 0), "y", axis=0)

    half = (16, ROWS, cols)
    normt, normed, query, keep, send = call(
        lambda *refs: first_kernel(scale, *refs),
        [((2, 16, ROWS, count), BF16), ((count, model_width), BF16), ((count, cols), F32), (half, BF16), (half, BF16)],
        smem=1,
    )(at, both, w_own, w_oth, keys, values, cotangent)

    first = scatter_dp(keep, send)
    own, oth = gather_dp(first.astype(BF16))
    move, square = call(project_kernel, [((count, cols), F32), ((8, HEAD), F32)])(normed, own, oth)
    square = lax.all_to_all(jnp.broadcast_to(square, (16, *square.shape)), ("y", "zh"), 0, 0, tiled=True)
    keep, send = call(
        lambda *refs: second_kernel(scale, radius, *refs), [(half, BF16), (half, BF16)]
    )(square, query, move, normt, keys, values, cotangent)
    return scatter_dp(keep, send)


def solution(mesh):
    cut = Mesh(mesh.devices.reshape(SIZES), AXES)
    spec = P(("zl", "x", "core"), ("y", "zh"))
    return jax.shard_map(shards, mesh=cut, in_specs=(spec,) * 5, out_specs=spec, check_vma=False)
```

```python
import math

import jax
import jax.numpy as jnp
from jax import lax
from jax.experimental import pallas as pl
from jax.experimental.pallas import tpu as pltpu
from jax.sharding import Mesh, PartitionSpec as P

HEAD = 128
ROWS = 96
EPS = 1e-06
F32 = jnp.float32
BF16 = jnp.bfloat16
AXES = ("zl", "x", "core", "y", "zh")
SIZES = (4, 4, 2, 8, 2)
STEPS = (0, -1, 1, -2, 2, -3, 3, -4)
VMEM_LIMIT = 48 * 1024 * 1024


def mm(a, b, dims=((1,), (0,))):
    return lax.dot_general(a, b, (dims, ((), ())), preferred_element_type=F32)


def query_grad(query, keys, values, cotangent):
    temper = 1.0 / math.sqrt(HEAD)
    heads = []
    for h in range(query.shape[1] // HEAD):
        cols = slice(h * HEAD, (h + 1) * HEAD)
        q = query[:, cols]
        key, value, cot = keys[:, cols], values[:, cols], cotangent[:, cols]
        center = q - jnp.mean(q, -1, keepdims=True)
        inverse = lax.rsqrt(jnp.mean(center * center, -1, keepdims=True) + EPS)
        qn = center * inverse
        scores = mm(qn.astype(BF16), key, ((1,), (1,))) * temper
        expon = jnp.exp(scores)
        attend = expon / jnp.sum(expon, -1, keepdims=True)
        dprob = mm(cot, value, ((1,), (1,)))
        dscore = attend * (dprob - jnp.sum(attend * dprob, -1, keepdims=True))
        dqn = mm(dscore.astype(BF16), key) * temper
        dq = inverse * (
            dqn
            - jnp.mean(dqn, -1, keepdims=True)
            - qn * jnp.mean(dqn * qn, -1, keepdims=True)
        )
        heads.append(dq.astype(BF16))
    return jnp.concatenate(heads, axis=1)


def first_kernel(scale, at_ref, *refs):
    toks, (w_ref, keys_ref, values_ref, cot_ref, normt_ref, normed_ref, query_ref, keep_ref, send_ref) = refs[:8], refs[8:]
    core, y, zh = at_ref[0], at_ref[1], at_ref[2]
    width = normed_ref.shape[1]
    total = jnp.zeros((1, normt_ref.shape[-1]), F32)
    for ref in toks:
        total += jnp.sum(ref[...].astype(F32), 0, keepdims=True)
    mean = total / width
    total = jnp.zeros_like(total)
    for ref in toks:
        center = ref[...].astype(F32) - mean
        total += jnp.sum(center * center, 0, keepdims=True)
    inverse = lax.rsqrt(total / width + EPS)
    for ref, step in zip(toks, STEPS):
        block = ((ref[...].astype(F32) - mean) * inverse).astype(BF16)
        from_y = lax.rem(y + (step + 8), 8)
        for part in range(4):
            x = 2 * lax.rem(from_y, 2) + jnp.bitwise_xor(zh, part // 2)
            normt_ref[part % 2, x, from_y // 2] = block[part * ROWS:(part + 1) * ROWS]
    run = 4 * ROWS
    for x in range(4):
        for c in range(2):
            at = (2 * x + c) * run
            normed_ref[:, at:at + run] = normt_ref[c, x].reshape(run, normt_ref.shape[-1]).T
    query = mm(normed_ref[...], w_ref[...])
    query_ref[...] = query
    dq = query_grad(query, keys_ref[...], values_ref[...], cot_ref[...])
    term(scale, core, normt_ref, dq, keep_ref, send_ref)


def term(scale, core, normt_ref, dq, keep_ref, send_ref):
    for c, ref in ((core, keep_ref), (1 - core, send_ref)):
        rows = normt_ref[c].reshape(16 * ROWS, normt_ref.shape[-1])
        ref[...] = (mm(rows, dq) * scale).astype(BF16).reshape(ref.shape)


def sum_kernel(parts_ref, first_ref, square_ref):
    total = jnp.sum(parts_ref[...].astype(F32), 0)
    first_ref[...] = total.astype(BF16)
    square = jnp.sum((total * total).reshape(-1, 8, total.shape[1]), 0)
    square_ref[...] = square[:, :HEAD] + square[:, HEAD:]


def second_kernel(scale, radius, at_ref, square_ref, query_ref, first_ref, normed_ref, normt_ref, keys_ref, values_ref,
                  cot_ref, keep_ref, send_ref):
    norm = jnp.sqrt(jnp.sum(jnp.sum(square_ref[...], 0), keepdims=True))
    query = query_ref[...] + (radius / norm) * mm(normed_ref[...], first_ref[...])
    dq = query_grad(query, keys_ref[...], values_ref[...], cot_ref[...])
    term(scale, at_ref[0], normt_ref, dq, keep_ref, send_ref)


def call(kernel, outs, smem=0):
    spec = pl.BlockSpec(memory_space=pltpu.VMEM)

    def run(*args):
        specs = [pl.BlockSpec(memory_space=pltpu.SMEM)] * smem + [spec] * (len(args) - smem)
        return pl.pallas_call(
            kernel,
            out_shape=[jax.ShapeDtypeStruct(s, d) for s, d in outs],
            in_specs=specs,
            out_specs=[spec] * len(outs),
            compiler_params=pltpu.CompilerParams(vmem_limit_bytes=VMEM_LIMIT),
        )(*args)

    return run


def swap(size, step):
    return [(i, i ^ step) for i in range(size)]


def turn(value, step):
    return lax.ppermute(value, "y", [(i, (i + step) % 8) for i in range(8)])


def after(value, *others):
    return lax.optimization_barrier((value, *others))[0]


def gather_tokens(block):
    back1, ahead1, back2, ahead2 = turn(block, 1), turn(block, 7), turn(block, 2), turn(block, 6)
    back3, ahead3, back4 = turn(back2, 1), turn(ahead2, 7), turn(back2, 2)
    return block, back1, ahead1, back2, ahead2, back3, ahead3, back4


def scatter_parts(keep, send):
    got = lax.ppermute(send, "core", swap(2, 1))
    both = (keep.astype(F32) + got.astype(F32)).astype(BF16)
    return lax.all_to_all(both, ("x", "zl"), 0, 0, tiled=True)


def everywhere(value, axes, size):
    return lax.all_to_all(jnp.broadcast_to(value, (size, *value.shape)), axes, 0, 0, tiled=True)


def shards(tokens, keys, values, cotangent, query_weight):
    tok = tokens.T
    feats, count = tok.shape
    cols = keys.shape[1]
    model_width = feats * 16
    scale = 1.0 / math.sqrt(count * 32)
    radius = 0.3 * math.sqrt(model_width + cols * 16)
    at = jnp.stack([lax.axis_index(name) for name in ("core", "y", "zh")]).astype(jnp.int32)

    other = lax.ppermute(tok, "zh", swap(2, 1))
    weight_z = lax.all_gather(query_weight, "zl", axis=0, tiled=True)
    weight_z, other = lax.optimization_barrier((weight_z, other))
    weight = lax.all_gather(weight_z, ("x", "core"), axis=0, tiled=True)
    blocks = gather_tokens(jnp.concatenate([tok, other], 0))

    half = (16, ROWS, cols)
    normt, normed, query, keep, send = call(
        lambda *refs: first_kernel(scale, *refs),
        [((2, 4, 4, ROWS, count), BF16), ((count, model_width), BF16), ((count, cols), F32), (half, BF16), (half, BF16)],
        smem=1,
    )(at, *blocks, weight, keys, values, cotangent)

    first, square = call(sum_kernel, [((ROWS, cols), BF16), ((8, HEAD), F32)])(scatter_parts(keep, send))
    first_z = lax.all_gather(first, "zl", axis=0, tiled=True)
    first_all = lax.all_gather(first_z, ("x", "core"), axis=0, tiled=True)
    square = jnp.sum(everywhere(after(square, first_z), ("zh", "y"), 16), 0)
    square = everywhere(square, ("zl", "x", "core"), 32)
    keep, send = call(
        lambda *refs: second_kernel(scale, radius, *refs), [(half, BF16), (half, BF16)], smem=1
    )(at, square, query, first_all, normed, normt, keys, values, cotangent)
    return jnp.sum(scatter_parts(keep, send).astype(F32), 0)


def solution(mesh):
    cut = Mesh(mesh.devices.reshape(SIZES), AXES)
    spec = P(("zl", "x", "core"), ("y", "zh"))
    return jax.shard_map(shards, mesh=cut, in_specs=(spec,) * 5, out_specs=spec, check_vma=False)
```

```python
import math

import jax
import jax.numpy as jnp
from jax import lax
from jax.experimental import pallas as pl
from jax.experimental.pallas import tpu as pltpu
from jax.sharding import Mesh, PartitionSpec as P

HEAD = 128
ROWS = 96
EPS = 1e-06
F32 = jnp.float32
BF16 = jnp.bfloat16
AXES = ("zl", "x", "core", "y", "zh")
SIZES = (4, 4, 2, 8, 2)
STEPS = (0, -1, 1, -2, 2, -3, 3, -4)


def mm(a, b, dims=((1,), (0,))):
    return lax.dot_general(a, b, (dims, ((), ())), preferred_element_type=F32)


def query_grad(query, keys, values, cotangent):
    temper = 1.0 / math.sqrt(HEAD)
    heads = []
    for h in range(query.shape[1] // HEAD):
        cols = slice(h * HEAD, (h + 1) * HEAD)
        q = query[:, cols]
        key, value, cot = keys[:, cols], values[:, cols], cotangent[:, cols]
        center = q - jnp.mean(q, -1, keepdims=True)
        inverse = lax.rsqrt(jnp.mean(center * center, -1, keepdims=True) + EPS)
        qn = center * inverse
        scores = mm(qn.astype(BF16), key, ((1,), (1,))) * temper
        expon = jnp.exp(scores)
        attend = expon / jnp.sum(expon, -1, keepdims=True)
        dprob = mm(cot, value, ((1,), (1,)))
        dscore = attend * (dprob - jnp.sum(attend * dprob, -1, keepdims=True))
        dqn = mm(dscore.astype(BF16), key) * temper
        dq = inverse * (
            dqn
            - jnp.mean(dqn, -1, keepdims=True)
            - qn * jnp.mean(dqn * qn, -1, keepdims=True)
        )
        heads.append(dq.astype(BF16))
    return jnp.concatenate(heads, axis=1)


def fetch(pairs, sems):
    copies = [pltpu.make_async_copy(src, dst, sems.at[i]) for i, (src, dst) in enumerate(pairs)]
    for copy in copies:
        copy.start()
    return copies


def wait(copies):
    for copy in copies:
        copy.wait()


def by_zl(src_ref, dst_ref):
    zl = lax.axis_index("zl")
    return [(src_ref.at[:, k, :ROWS], dst_ref.at[:, jnp.bitwise_xor(zl, k)]) for k in range(4)]


def first_kernel(scale, *refs):
    toks, refs = refs[:8], refs[8:]
    w_any, sides_any, normt_ref, normed_ref, query_ref, keep_ref, send_ref, w_ref, sides_ref, sems = refs
    copies = fetch(by_zl(w_any, w_ref) + [(sides_any, sides_ref)], sems)
    y, zh = lax.axis_index("y"), lax.axis_index("zh")
    width = normed_ref.shape[1]
    total = jnp.zeros((1, normt_ref.shape[-1]), F32)
    for ref in toks:
        total += jnp.sum(ref[...].astype(F32), 0, keepdims=True)
    mean = total / width
    total = jnp.zeros_like(total)
    for ref in toks:
        center = ref[...].astype(F32) - mean
        total += jnp.sum(center * center, 0, keepdims=True)
    inverse = lax.rsqrt(total / width + EPS)
    for ref, step in zip(toks, STEPS):
        block = ((ref[...].astype(F32) - mean) * inverse).astype(BF16)
        from_y = lax.rem(y + (step + 8), 8)
        for part in range(4):
            x = 2 * lax.rem(from_y, 2) + jnp.bitwise_xor(zh, part // 2)
            normt_ref[part % 2, x, from_y // 2] = block[part * ROWS:(part + 1) * ROWS]
    run = 4 * ROWS
    for x in range(4):
        for c in range(2):
            at = (2 * x + c) * run
            normed_ref[:, at:at + run] = normt_ref[c, x].reshape(run, normt_ref.shape[-1]).T
    wait(copies)
    query = mm(normed_ref[...], w_ref[...].reshape(width, w_ref.shape[-1]))
    query_ref[...] = query
    dq = query_grad(query, sides_ref[0], sides_ref[1], sides_ref[2])
    term(scale, normt_ref, dq, keep_ref, send_ref)


def term(scale, normt_ref, dq, keep_ref, send_ref):
    core = lax.axis_index("core")
    for c, ref in ((core, keep_ref), (1 - core, send_ref)):
        rows = normt_ref[c].reshape(16 * ROWS, normt_ref.shape[-1])
        ref[...] = (mm(rows, dq) * scale).astype(BF16).reshape(ref.shape)


def sum_kernel(parts_ref, out_ref):
    total = jnp.sum(parts_ref[...].astype(F32), 0)
    square = jnp.sum((total * total).reshape(-1, 8, total.shape[1]), 0)
    high = square.astype(BF16)
    out_ref[:ROWS] = total.astype(BF16)
    out_ref[ROWS:] = jnp.concatenate([high.astype(F32), square - high.astype(F32)], 0).astype(BF16)


def second_kernel(scale, radius, square_any, query_any, first_any, normed_any, normt_any, sides_any,
                  keep_ref, send_ref, square_ref, query_ref, first_ref, normed_ref, normt_ref, sides_ref, sems):
    pairs = by_zl(first_any, first_ref) + [(normed_any, normed_ref), (square_any, square_ref)]
    pairs += [(query_any, query_ref), (sides_any, sides_ref), (normt_any, normt_ref)]
    copies = fetch(pairs, sems)
    wait(copies[:5])
    move = mm(normed_ref[...], first_ref[...].reshape(normed_ref.shape[1], first_ref.shape[-1]))
    wait(copies[5:8])
    norm = jnp.sqrt(jnp.sum(jnp.sum(square_ref[...], 0), keepdims=True))
    query = query_ref[...] + (radius / norm) * move
    dq = query_grad(query, sides_ref[0], sides_ref[1], sides_ref[2])
    wait(copies[8:])
    term(scale, normt_ref, dq, keep_ref, send_ref)


def call(kernel, outs, limit, anywhere=(), scratch=()):
    spec = pl.BlockSpec(memory_space=pltpu.VMEM)

    def run(*args):
        return pl.pallas_call(
            kernel,
            out_shape=[jax.ShapeDtypeStruct(s, d) for s, d in outs],
            in_specs=[pl.BlockSpec(memory_space=pl.ANY) if i in anywhere else spec for i in range(len(args))],
            out_specs=[spec] * len(outs),
            scratch_shapes=list(scratch),
            compiler_params=pltpu.CompilerParams(vmem_limit_bytes=limit * 1024 * 1024),
        )(*args)

    return run


def swap(size, step):
    return [(i, i ^ step) for i in range(size)]


def turn(value, step):
    return lax.ppermute(value, "y", [(i, (i + step) % 8) for i in range(8)])


def after(value, *others):
    return lax.optimization_barrier((value, *others))[0]


def gather_tokens(block):
    back1, ahead1, back2, ahead2 = turn(block, 1), turn(block, 7), turn(block, 2), turn(block, 6)
    back3, ahead3, back4 = turn(back2, 1), turn(ahead2, 7), turn(back2, 2)
    return block, back1, ahead1, back2, ahead2, back3, ahead3, back4


def scatter_parts(keep, send):
    got = lax.ppermute(send, "core", swap(2, 1))
    both = (keep.astype(F32) + got.astype(F32)).astype(BF16)
    return lax.all_to_all(both, ("x", "zl"), 0, 0, tiled=True)


def everywhere(value, axes, size):
    return lax.all_to_all(jnp.broadcast_to(value, (size, *value.shape)), axes, 0, 0, tiled=True)


def gather_z(block):
    return jnp.stack([block] + [lax.ppermute(block, "zl", swap(4, k)) for k in (1, 2, 3)])


def gather_chips(blocks):
    return lax.all_gather(blocks, ("x", "core"), axis=0)


def shards(tokens, keys, values, cotangent, query_weight):
    tok = tokens.T
    feats, count = tok.shape
    cols = keys.shape[1]
    model_width = feats * 16
    scale = 1.0 / math.sqrt(count * 32)
    radius = 0.3 * math.sqrt(model_width + cols * 16)
    whole, half = (8, 4, ROWS, cols), (16, ROWS, cols)
    normt_like = (2, 4, 4, ROWS, count)
    sides = jnp.stack([keys, values, cotangent])

    other = lax.ppermute(tok, "zh", swap(2, 1))
    weight_z, other = lax.optimization_barrier((gather_z(query_weight), other))
    weight = gather_chips(weight_z)
    blocks = gather_tokens(jnp.concatenate([tok, other], 0))

    normt, normed, query, keep, send = call(
        lambda *refs: first_kernel(scale, *refs),
        [(normt_like, BF16), ((count, model_width), BF16), ((count, cols), F32), (half, BF16), (half, BF16)],
        48,
        anywhere=(8, 9),
        scratch=(pltpu.VMEM(whole, BF16), pltpu.VMEM(sides.shape, BF16), pltpu.SemaphoreType.DMA((5,))),
    )(*blocks, weight, sides)

    first = call(sum_kernel, [((ROWS + 16, cols), BF16)], 48)(scatter_parts(keep, send))[0]
    first_z = gather_z(first)
    first_all = gather_chips(first_z)
    square = jnp.sum(first_z[:, ROWS:].astype(F32).reshape(8, 8, 2, HEAD), (0, 2))
    square = jnp.sum(everywhere(square, ("zh", "y"), 16), 0)
    square = everywhere(square, ("x", "core"), 8)
    args = (square, query, first_all, normed, normt, sides)
    keep, send = call(
        lambda *refs: second_kernel(scale, radius, *refs),
        [(half, BF16), (half, BF16)],
        58,
        anywhere=range(len(args)),
        scratch=[pltpu.VMEM(whole if arg is first_all else arg.shape, arg.dtype) for arg in args]
        + [pltpu.SemaphoreType.DMA((9,))],
    )(*args)
    return jnp.sum(scatter_parts(keep, send).astype(F32), 0)


def solution(mesh):
    cut = Mesh(mesh.devices.reshape(SIZES), AXES)
    spec = P(("zl", "x", "core"), ("y", "zh"))
    return jax.shard_map(shards, mesh=cut, in_specs=(spec,) * 5, out_specs=spec, check_vma=False)
```

```python
import math

import jax
import jax.numpy as jnp
from jax import lax
from jax.experimental import pallas as pl
from jax.experimental.pallas import tpu as pltpu
from jax.sharding import Mesh, PartitionSpec as P

HEAD = 128
ROWS = 96
EPS = 1e-06
F32 = jnp.float32
BF16 = jnp.bfloat16
AXES = ("zl", "x", "core", "y", "zh")
SIZES = (4, 4, 2, 8, 2)
STEPS = (0, -1, 1, -2, 2, -3, 3, -4)


def mm(a, b, dims=((1,), (0,))):
    return lax.dot_general(a, b, (dims, ((), ())), preferred_element_type=F32)


def query_grad(query, keys, values, cotangent):
    temper = 1.0 / math.sqrt(HEAD)
    heads = []
    for h in range(query.shape[1] // HEAD):
        cols = slice(h * HEAD, (h + 1) * HEAD)
        q = query[:, cols]
        key, value, cot = keys[:, cols], values[:, cols], cotangent[:, cols]
        center = q - jnp.mean(q, -1, keepdims=True)
        inverse = lax.rsqrt(jnp.mean(center * center, -1, keepdims=True) + EPS)
        qn = center * inverse
        scores = mm(qn.astype(BF16), key, ((1,), (1,))) * temper
        expon = jnp.exp(scores)
        attend = expon / jnp.sum(expon, -1, keepdims=True)
        dprob = mm(cot, value, ((1,), (1,)))
        dscore = attend * (dprob - jnp.sum(attend * dprob, -1, keepdims=True))
        dqn = mm(dscore.astype(BF16), key) * temper
        dq = inverse * (
            dqn
            - jnp.mean(dqn, -1, keepdims=True)
            - qn * jnp.mean(dqn * qn, -1, keepdims=True)
        )
        heads.append(dq.astype(BF16))
    return jnp.concatenate(heads, axis=1)


def fetch(pairs, sems):
    copies = [pltpu.make_async_copy(src, dst, sems.at[i]) for i, (src, dst) in enumerate(pairs)]
    for copy in copies:
        copy.start()
    return copies


def wait(copies):
    for copy in copies:
        copy.wait()


def by_zl(src_ref, dst_ref):
    zl = lax.axis_index("zl")
    return [(src_ref.at[:, k, :ROWS], dst_ref.at[:, jnp.bitwise_xor(zl, k)]) for k in range(4)]


def first_kernel(scale, *refs):
    toks, refs = refs[:8], refs[8:]
    w_any, sides_any, normt_ref, normed_ref, query_ref, keep_ref, send_ref, w_ref, sides_ref, sems = refs
    copies = fetch(by_zl(w_any, w_ref) + [(sides_any, sides_ref)], sems)
    y, zh = lax.axis_index("y"), lax.axis_index("zh")
    width = normed_ref.shape[1]
    total = jnp.zeros((1, normt_ref.shape[-1]), F32)
    for ref in toks:
        total += jnp.sum(ref[...].astype(F32), 0, keepdims=True)
    mean = total / width
    total = jnp.zeros_like(total)
    for ref in toks:
        center = ref[...].astype(F32) - mean
        total += jnp.sum(center * center, 0, keepdims=True)
    inverse = lax.rsqrt(total / width + EPS)
    for ref, step in zip(toks, STEPS):
        block = ((ref[...].astype(F32) - mean) * inverse).astype(BF16)
        from_y = lax.rem(y + (step + 8), 8)
        for part in range(4):
            x = 2 * lax.rem(from_y, 2) + jnp.bitwise_xor(zh, part // 2)
            normt_ref[part % 2, x, from_y // 2] = block[part * ROWS:(part + 1) * ROWS]
    run = 4 * ROWS
    for x in range(4):
        for c in range(2):
            at = (2 * x + c) * run
            normed_ref[:, at:at + run] = normt_ref[c, x].reshape(run, normt_ref.shape[-1]).T
    wait(copies)
    query = mm(normed_ref[...], w_ref[...].reshape(width, w_ref.shape[-1]))
    query_ref[...] = query
    dq = query_grad(query, sides_ref[0], sides_ref[1], sides_ref[2])
    term(scale, normt_ref, dq, keep_ref, send_ref)


def term(scale, normt_ref, dq, keep_ref, send_ref):
    core = lax.axis_index("core")
    for c, ref in ((core, keep_ref), (1 - core, send_ref)):
        rows = normt_ref[c].reshape(16 * ROWS, normt_ref.shape[-1])
        ref[...] = (mm(rows, dq) * scale).astype(BF16).reshape(ref.shape)


def sum_kernel(parts_ref, out_ref):
    out_ref[...] = jnp.sum(parts_ref[...].astype(F32), 0).astype(BF16)


def last_sum_kernel(*refs):
    parts, (first_ref, square_ref) = refs[:4], refs[4:]
    total = sum(ref[...].astype(F32) for ref in parts)
    first_ref[...] = total.astype(BF16)
    square = jnp.sum((total * total).reshape(-1, 8, total.shape[1]), 0)
    square_ref[...] = square[:, :HEAD] + square[:, HEAD:]


def second_kernel(scale, radius, square_ref, query_ref, first_ref, normed_ref, normt_any, sides_ref,
                  keep_ref, send_ref, normt_ref, sems):
    copies = fetch([(normt_any, normt_ref)], sems)
    norm = jnp.sqrt(jnp.sum(jnp.sum(square_ref[...], 0), keepdims=True))
    move = mm(normed_ref[...], first_ref[...].reshape(normed_ref.shape[1], first_ref.shape[-1]))
    query = query_ref[...] + (radius / norm) * move
    dq = query_grad(query, sides_ref[0], sides_ref[1], sides_ref[2])
    wait(copies)
    term(scale, normt_ref, dq, keep_ref, send_ref)


def call(kernel, outs, limit, anywhere=(), scratch=()):
    spec = pl.BlockSpec(memory_space=pltpu.VMEM)

    def run(*args):
        return pl.pallas_call(
            kernel,
            out_shape=[jax.ShapeDtypeStruct(s, d) for s, d in outs],
            in_specs=[pl.BlockSpec(memory_space=pl.ANY) if i in anywhere else spec for i in range(len(args))],
            out_specs=[spec] * len(outs),
            scratch_shapes=list(scratch),
            compiler_params=pltpu.CompilerParams(vmem_limit_bytes=limit * 1024 * 1024),
        )(*args)

    return run


def swap(size, step):
    return [(i, i ^ step) for i in range(size)]


def turn(value, step):
    return lax.ppermute(value, "y", [(i, (i + step) % 8) for i in range(8)])


def after(value, *others):
    return lax.optimization_barrier((value, *others))[0]


def gather_tokens(block):
    back1, ahead1, back2, ahead2 = turn(block, 1), turn(block, 7), turn(block, 2), turn(block, 6)
    back3, ahead3, back4 = turn(back2, 1), turn(ahead2, 7), turn(back2, 2)
    return block, back1, ahead1, back2, ahead2, back3, ahead3, back4


def sum_core(keep, send):
    got = lax.ppermute(send, "core", swap(2, 1))
    return (keep.astype(F32) + got.astype(F32)).astype(BF16)


def everywhere(value, axes, size):
    return lax.all_to_all(jnp.broadcast_to(value, (size, *value.shape)), axes, 0, 0, tiled=True)


def along_z(block):
    return [block] + [lax.ppermute(block, "zl", swap(4, k)) for k in (1, 2, 3)]


def gather_chips(blocks):
    return lax.all_gather(blocks, ("x", "core"), axis=0)


def shards(tokens, keys, values, cotangent, query_weight):
    tok = tokens.T
    feats, count = tok.shape
    cols = keys.shape[1]
    model_width = feats * 16
    scale = 1.0 / math.sqrt(count * 32)
    radius = 0.3 * math.sqrt(model_width + cols * 16)
    whole, half = (8, 4, ROWS, cols), (16, ROWS, cols)
    normt_like = (2, 4, 4, ROWS, count)
    sides = jnp.stack([keys, values, cotangent])

    other = lax.ppermute(tok, "zh", swap(2, 1))
    weight_z = along_z(query_weight)
    *weight_z, other = lax.optimization_barrier((*weight_z, other))
    weight_z = jnp.stack(weight_z)
    weight = gather_chips(weight_z)
    blocks = gather_tokens(jnp.concatenate([tok, other], 0))

    normt, normed, query, keep, send = call(
        lambda *refs: first_kernel(scale, *refs),
        [(normt_like, BF16), ((count, model_width), BF16), ((count, cols), F32), (half, BF16), (half, BF16)],
        48,
        anywhere=(8, 9),
        scratch=(pltpu.VMEM(whole, BF16), pltpu.VMEM(sides.shape, BF16), pltpu.SemaphoreType.DMA((5,))),
    )(*blocks, weight, sides)

    quarter = (4 * ROWS, cols)
    parts = lax.all_to_all(sum_core(keep, send).reshape(4, *quarter), "x", 0, 0, tiled=True)
    partial = call(sum_kernel, [(quarter, BF16)], 48)(parts)[0]
    first, square = call(last_sum_kernel, [(quarter, BF16), ((8, HEAD), F32)], 48)(*along_z(partial))
    first_all = gather_chips(first)
    square = jnp.sum(everywhere(square, ("zh", "y"), 16), 0)
    square = everywhere(square, ("x", "core"), 8)
    keep, send = call(
        lambda *refs: second_kernel(scale, radius, *refs),
        [(half, BF16), (half, BF16)],
        48,
        anywhere=(4,),
        scratch=(pltpu.VMEM(normt_like, BF16), pltpu.SemaphoreType.DMA((1,))),
    )(square, query, first_all, normed, normt, sides)
    parts = lax.all_to_all(sum_core(keep, send), ("x", "zl"), 0, 0, tiled=True)
    return jnp.sum(parts.astype(F32), 0)


def solution(mesh):
    cut = Mesh(mesh.devices.reshape(SIZES), AXES)
    spec = P(("zl", "x", "core"), ("y", "zh"))
    return jax.shard_map(shards, mesh=cut, in_specs=(spec,) * 5, out_specs=spec, check_vma=False)
```

```python
import math

import jax
import jax.numpy as jnp
from jax import lax
from jax.experimental import pallas as pl
from jax.experimental.pallas import tpu as pltpu
from jax.sharding import Mesh, PartitionSpec as P

HEAD = 128
ROWS = 96
EPS = 1e-06
F32 = jnp.float32
BF16 = jnp.bfloat16
AXES = ("z2", "z1", "x", "core", "y", "zh")
SIZES = (2, 2, 4, 2, 8, 2)
STEPS = (0, -1, 1, -2, 2, -3, 3, -4)


def mm(a, b, dims=((1,), (0,))):
    return lax.dot_general(a, b, (dims, ((), ())), preferred_element_type=F32)


def query_grad(query, keys, values, cotangent):
    temper = 1.0 / math.sqrt(HEAD)
    heads = []
    for h in range(query.shape[1] // HEAD):
        cols = slice(h * HEAD, (h + 1) * HEAD)
        q = query[:, cols]
        key, value, cot = keys[:, cols], values[:, cols], cotangent[:, cols]
        center = q - jnp.mean(q, -1, keepdims=True)
        inverse = lax.rsqrt(jnp.mean(center * center, -1, keepdims=True) + EPS)
        qn = center * inverse
        scores = mm(qn.astype(BF16), key, ((1,), (1,))) * temper
        expon = jnp.exp(scores)
        attend = expon / jnp.sum(expon, -1, keepdims=True)
        dprob = mm(cot, value, ((1,), (1,)))
        dscore = attend * (dprob - jnp.sum(attend * dprob, -1, keepdims=True))
        dqn = mm(dscore.astype(BF16), key) * temper
        dq = inverse * (
            dqn
            - jnp.mean(dqn, -1, keepdims=True)
            - qn * jnp.mean(dqn * qn, -1, keepdims=True)
        )
        heads.append(dq.astype(BF16))
    return jnp.concatenate(heads, axis=1)


def fetch(pairs, sems):
    copies = [pltpu.make_async_copy(src, dst, sems.at[i]) for i, (src, dst) in enumerate(pairs)]
    for copy in copies:
        copy.start()
    return copies


def wait(copies):
    for copy in copies:
        copy.wait()


def by_z(src_ref, dst_ref):
    z1, z2 = lax.axis_index("z1"), lax.axis_index("z2")
    return [
        (src_ref.at[:, k], dst_ref.at[:, jnp.bitwise_xor(z1, k % 2), jnp.bitwise_xor(z2, k // 2)]) for k in range(4)
    ]


def first_kernel(scale, *refs):
    toks, refs = refs[:8], refs[8:]
    w_any, sides_any, normt_ref, normed_ref, query_ref, keep_ref, send_ref, w_ref, sides_ref, sems = refs
    copies = fetch(by_z(w_any, w_ref) + [(sides_any, sides_ref)], sems)
    y, zh = lax.axis_index("y"), lax.axis_index("zh")
    width = normed_ref.shape[1]
    total = jnp.zeros((1, normt_ref.shape[-1]), F32)
    for ref in toks:
        total += jnp.sum(ref[...].astype(F32), 0, keepdims=True)
    mean = total / width
    total = jnp.zeros_like(total)
    for ref in toks:
        center = ref[...].astype(F32) - mean
        total += jnp.sum(center * center, 0, keepdims=True)
    inverse = lax.rsqrt(total / width + EPS)
    for ref, step in zip(toks, STEPS):
        block = ((ref[...].astype(F32) - mean) * inverse).astype(BF16)
        from_y = lax.rem(y + (step + 8), 8)
        for part in range(4):
            x = 2 * lax.rem(from_y, 2) + jnp.bitwise_xor(zh, part // 2)
            normt_ref[part % 2, x, lax.rem(from_y // 2, 2), from_y // 4] = block[part * ROWS:(part + 1) * ROWS]
    run = 4 * ROWS
    for x in range(4):
        for c in range(2):
            at = (2 * x + c) * run
            normed_ref[:, at:at + run] = normt_ref[c, x].reshape(run, normt_ref.shape[-1]).T
    wait(copies)
    query = mm(normed_ref[...], w_ref[...].reshape(width, w_ref.shape[-1]))
    query_ref[...] = query
    dq = query_grad(query, sides_ref[0], sides_ref[1], sides_ref[2])
    term(scale, normt_ref, dq, keep_ref, send_ref)


def term(scale, normt_ref, dq, keep_ref, send_ref):
    core = lax.axis_index("core")
    for c, ref in ((core, keep_ref), (1 - core, send_ref)):
        rows = normt_ref[c].reshape(16 * ROWS, normt_ref.shape[-1])
        ref[...] = (mm(rows, dq) * scale).astype(BF16).reshape(ref.shape)


def sum_kernel(parts_ref, out_ref):
    out_ref[...] = jnp.sum(parts_ref[...].astype(F32), 0).astype(BF16)


def half_sums_kernel(parts_ref, own_ref, give_ref):
    z2 = lax.axis_index("z2")
    own_ref[...] = jnp.sum(parts_ref[:, z2].astype(F32), 0)
    give_ref[...] = jnp.sum(parts_ref[:, 1 - z2].astype(F32), 0).astype(BF16)


def pair_kernel(mine_ref, theirs_ref, first_ref, square_ref):
    z1 = lax.axis_index("z1")
    first_ref[z1] = mine_ref[...]
    first_ref[1 - z1] = theirs_ref[...]
    mine, theirs = mine_ref[...].astype(F32), theirs_ref[...].astype(F32)
    square = jnp.sum((mine * mine + theirs * theirs).reshape(-1, 8, mine.shape[1]), 0)
    square_ref[...] = square[:, :HEAD] + square[:, HEAD:]


def second_kernel(scale, radius, square_ref, query_ref, first_ref, normed_ref, normt_any, sides_ref,
                  keep_ref, send_ref, normt_ref, sems):
    copies = fetch([(normt_any, normt_ref)], sems)
    norm = jnp.sqrt(jnp.sum(jnp.sum(square_ref[...], 0), keepdims=True))
    move = mm(normed_ref[...], first_ref[...].reshape(normed_ref.shape[1], first_ref.shape[-1]))
    query = query_ref[...] + (radius / norm) * move
    dq = query_grad(query, sides_ref[0], sides_ref[1], sides_ref[2])
    wait(copies)
    term(scale, normt_ref, dq, keep_ref, send_ref)


def call(kernel, outs, limit, anywhere=(), scratch=()):
    spec = pl.BlockSpec(memory_space=pltpu.VMEM)

    def run(*args):
        return pl.pallas_call(
            kernel,
            out_shape=[jax.ShapeDtypeStruct(s, d) for s, d in outs],
            in_specs=[pl.BlockSpec(memory_space=pl.ANY) if i in anywhere else spec for i in range(len(args))],
            out_specs=[spec] * len(outs),
            scratch_shapes=list(scratch),
            compiler_params=pltpu.CompilerParams(vmem_limit_bytes=limit * 1024 * 1024),
        )(*args)

    return run


def swap(size, step):
    return [(i, i ^ step) for i in range(size)]


def turn(value, step):
    return lax.ppermute(value, "y", [(i, (i + step) % 8) for i in range(8)])


def after(value, *others):
    return lax.optimization_barrier((value, *others))[0]


def gather_tokens(block):
    back1, ahead1, back2, ahead2 = turn(block, 1), turn(block, 7), turn(block, 2), turn(block, 6)
    back3, ahead3, back4 = turn(back2, 1), turn(ahead2, 7), turn(back2, 2)
    return block, back1, ahead1, back2, ahead2, back3, ahead3, back4


def add(a, b):
    return (a.astype(F32) + b.astype(F32)).astype(BF16)


def scatter_parts(keep, send):
    both = add(keep, lax.ppermute(send, "core", swap(2, 1)))
    pieces = both.reshape(8, 2 * ROWS, both.shape[-1])
    return lax.all_to_all(pieces, ("x", "z1"), 0, 0, tiled=True)


def everywhere(value, axes, size):
    return lax.all_to_all(jnp.broadcast_to(value, (size, *value.shape)), axes, 0, 0, tiled=True)


def along_z(block):
    return [block] + [lax.ppermute(block, ("z2", "z1"), swap(4, k)) for k in (1, 2, 3)]


def gather_chips(blocks):
    return lax.all_gather(blocks, ("x", "core"), axis=0)


def shards(tokens, keys, values, cotangent, query_weight):
    tok = tokens.T
    feats, count = tok.shape
    cols = keys.shape[1]
    model_width = feats * 16
    scale = 1.0 / math.sqrt(count * 32)
    radius = 0.3 * math.sqrt(model_width + cols * 16)
    whole, half = (8, 2, 2, ROWS, cols), (16, ROWS, cols)
    normt_like = (2, 4, 2, 2, ROWS, count)
    sides = jnp.stack([keys, values, cotangent])

    other = lax.ppermute(tok, "zh", swap(2, 1))
    weight_z = along_z(query_weight)
    *weight_z, other = lax.optimization_barrier((*weight_z, other))
    weight_z = jnp.stack(weight_z)
    weight = gather_chips(weight_z)
    blocks = gather_tokens(jnp.concatenate([tok, other], 0))

    normt, normed, query, keep, send = call(
        lambda *refs: first_kernel(scale, *refs),
        [(normt_like, BF16), ((count, model_width), BF16), ((count, cols), F32), (half, BF16), (half, BF16)],
        48,
        anywhere=(8, 9),
        scratch=(pltpu.VMEM(whole, BF16), pltpu.VMEM(sides.shape, BF16), pltpu.SemaphoreType.DMA((5,))),
    )(*blocks, weight, sides)

    pair = (2 * ROWS, cols)
    partial = call(sum_kernel, [(pair, BF16)], 48)(scatter_parts(keep, send))[0]
    mine = add(partial, lax.ppermute(partial, "z2", swap(2, 1)))
    theirs = lax.ppermute(mine, "z1", swap(2, 1))
    first, square = call(pair_kernel, [((2, *pair), BF16), ((8, HEAD), F32)], 48)(mine, theirs)
    first_all = gather_chips(first)
    square = jnp.sum(everywhere(square, ("zh", "y"), 16), 0)
    square = everywhere(square, ("x", "core"), 8)
    keep, send = call(
        lambda *refs: second_kernel(scale, radius, *refs),
        [(half, BF16), (half, BF16)],
        48,
        anywhere=(4,),
        scratch=(pltpu.VMEM(normt_like, BF16), pltpu.SemaphoreType.DMA((1,))),
    )(square, query, first_all, normed, normt, sides)
    parts = scatter_parts(keep, send).reshape(8, 2, ROWS, cols)
    own, give = call(half_sums_kernel, [((ROWS, cols), F32), ((ROWS, cols), BF16)], 48)(parts)
    return own + lax.ppermute(give, "z2", swap(2, 1)).astype(F32)


def solution(mesh):
    cut = Mesh(mesh.devices.reshape(SIZES), AXES)
    spec = P(AXES[:4], AXES[4:])
    return jax.shard_map(shards, mesh=cut, in_specs=(spec,) * 5, out_specs=spec, check_vma=False)
```

```python
import math

import jax
import jax.numpy as jnp
from jax import lax
from jax.experimental import pallas as pl
from jax.experimental.pallas import tpu as pltpu
from jax.sharding import Mesh, PartitionSpec as P

HEAD = 128
ROWS = 96
EPS = 1e-06
F32 = jnp.float32
BF16 = jnp.bfloat16
AXES = ("z2", "z1", "x", "core", "y", "zh")
SIZES = (2, 2, 4, 2, 8, 2)
STEPS = (0, -1, 1, -2, 2, -3, 3, 4)


def mm(a, b, dims=((1,), (0,))):
    return lax.dot_general(a, b, (dims, ((), ())), preferred_element_type=F32)


def query_grad(query, keys, values, cotangent):
    temper = 1.0 / math.sqrt(HEAD)
    heads = []
    for h in range(query.shape[1] // HEAD):
        cols = slice(h * HEAD, (h + 1) * HEAD)
        q = query[:, cols]
        key, value, cot = keys[:, cols], values[:, cols], cotangent[:, cols]
        center = q - jnp.mean(q, -1, keepdims=True)
        inverse = lax.rsqrt(jnp.mean(center * center, -1, keepdims=True) + EPS)
        qn = center * inverse
        scores = mm(qn.astype(BF16), key, ((1,), (1,))) * temper
        expon = jnp.exp(scores)
        attend = expon / jnp.sum(expon, -1, keepdims=True)
        dprob = mm(cot, value, ((1,), (1,)))
        dscore = attend * (dprob - jnp.sum(attend * dprob, -1, keepdims=True))
        dqn = mm(dscore.astype(BF16), key) * temper
        dq = inverse * (
            dqn
            - jnp.mean(dqn, -1, keepdims=True)
            - qn * jnp.mean(dqn * qn, -1, keepdims=True)
        )
        heads.append(dq.astype(BF16))
    return jnp.concatenate(heads, axis=1)


def fetch(pairs, sems):
    copies = [pltpu.make_async_copy(src, dst, sems.at[i]) for i, (src, dst) in enumerate(pairs)]
    for copy in copies:
        copy.start()
    return copies


def wait(copies):
    for copy in copies:
        copy.wait()


def by_z(src_ref, dst_ref):
    z1, z2 = lax.axis_index("z1"), lax.axis_index("z2")
    return [
        (src_ref.at[:, k], dst_ref.at[:, jnp.bitwise_xor(z1, k % 2), jnp.bitwise_xor(z2, k // 2)]) for k in range(4)
    ]


def first_kernel(scale, *refs):
    toks, refs = refs[:8], refs[8:]
    w_any, sides_any, normt_ref, normed_ref, query_ref, keep_ref, send_ref, w_ref, sides_ref, sems = refs
    copies = fetch(by_z(w_any, w_ref) + [(sides_any, sides_ref)], sems)
    y, zh = lax.axis_index("y"), lax.axis_index("zh")
    width = normed_ref.shape[1]
    total = jnp.zeros((1, normt_ref.shape[-1]), F32)
    for ref in toks:
        total += jnp.sum(ref[...].astype(F32), 0, keepdims=True)
    mean = total / width
    total = jnp.zeros_like(total)
    for ref in toks:
        center = ref[...].astype(F32) - mean
        total += jnp.sum(center * center, 0, keepdims=True)
    inverse = lax.rsqrt(total / width + EPS)
    for ref, step in zip(toks, STEPS):
        block = ((ref[...].astype(F32) - mean) * inverse).astype(BF16)
        from_y = lax.rem(y + (step + 8), 8)
        for part in range(4):
            x = 2 * lax.rem(from_y, 2) + jnp.bitwise_xor(zh, part // 2)
            normt_ref[part % 2, x, lax.rem(from_y // 2, 2), from_y // 4] = block[part * ROWS:(part + 1) * ROWS]
    run = 4 * ROWS
    for x in range(4):
        for c in range(2):
            at = (2 * x + c) * run
            normed_ref[:, at:at + run] = normt_ref[c, x].reshape(run, normt_ref.shape[-1]).T
    wait(copies)
    query = mm(normed_ref[...], w_ref[...].reshape(width, w_ref.shape[-1]))
    query_ref[...] = query
    dq = query_grad(query, sides_ref[0], sides_ref[1], sides_ref[2])
    term(scale, normt_ref, dq, keep_ref, send_ref)


def term(scale, normt_ref, dq, keep_ref, send_ref):
    core = lax.axis_index("core")
    for c, ref in ((core, keep_ref), (1 - core, send_ref)):
        rows = normt_ref[c].reshape(16 * ROWS, normt_ref.shape[-1])
        ref[...] = (mm(rows, dq) * scale).astype(BF16).reshape(ref.shape)


def sum_kernel(parts_ref, out_ref):
    out_ref[...] = jnp.sum(parts_ref[...].astype(F32), 0).astype(BF16)


def half_sums_kernel(parts_ref, own_ref, give_ref):
    z2 = lax.axis_index("z2")
    own_ref[...] = jnp.sum(parts_ref[:, z2].astype(F32), 0)
    give_ref[...] = jnp.sum(parts_ref[:, 1 - z2].astype(F32), 0).astype(BF16)


def pair_kernel(mine_ref, theirs_ref, first_ref, square_ref):
    z1 = lax.axis_index("z1")
    first_ref[z1] = mine_ref[...]
    first_ref[1 - z1] = theirs_ref[...]
    mine, theirs = mine_ref[...].astype(F32), theirs_ref[...].astype(F32)
    square = jnp.sum((mine * mine + theirs * theirs).reshape(-1, 8, mine.shape[1]), 0)
    square_ref[...] = square[:, :HEAD] + square[:, HEAD:]


def second_kernel(scale, radius, square_ref, query_ref, first_ref, normed_ref, normt_any, sides_ref,
                  keep_ref, send_ref, normt_ref, sems):
    copies = fetch([(normt_any, normt_ref)], sems)
    norm = jnp.sqrt(jnp.sum(jnp.sum(square_ref[...], 0), keepdims=True))
    move = mm(normed_ref[...], first_ref[...].reshape(normed_ref.shape[1], first_ref.shape[-1]))
    query = query_ref[...] + (radius / norm) * move
    dq = query_grad(query, sides_ref[0], sides_ref[1], sides_ref[2])
    wait(copies)
    term(scale, normt_ref, dq, keep_ref, send_ref)


def call(kernel, outs, limit, anywhere=(), scratch=()):
    spec = pl.BlockSpec(memory_space=pltpu.VMEM)

    def run(*args):
        return pl.pallas_call(
            kernel,
            out_shape=[jax.ShapeDtypeStruct(s, d) for s, d in outs],
            in_specs=[pl.BlockSpec(memory_space=pl.ANY) if i in anywhere else spec for i in range(len(args))],
            out_specs=[spec] * len(outs),
            scratch_shapes=list(scratch),
            compiler_params=pltpu.CompilerParams(vmem_limit_bytes=limit * 1024 * 1024),
        )(*args)

    return run


def swap(size, step):
    return [(i, i ^ step) for i in range(size)]


def turn(value, step):
    return lax.ppermute(value, "y", [(i, (i + step) % 8) for i in range(8)])


def after(value, *others):
    return lax.optimization_barrier((value, *others))[0]


def gather_tokens(block):
    back1, ahead1, back2, ahead2 = turn(block, 1), turn(block, 7), turn(block, 2), turn(block, 6)
    back3, ahead3, ahead4 = turn(back2, 1), turn(ahead2, 7), turn(ahead2, 6)
    return block, back1, ahead1, back2, ahead2, back3, ahead3, ahead4


def add(a, b):
    return (a.astype(F32) + b.astype(F32)).astype(BF16)


def scatter_parts(keep, send):
    both = add(keep, lax.ppermute(send, "core", swap(2, 1)))
    pieces = both.reshape(8, 2 * ROWS, both.shape[-1])
    return lax.all_to_all(pieces, ("x", "z1"), 0, 0, tiled=True)


def everywhere(value, axes, size):
    return lax.all_to_all(jnp.broadcast_to(value, (size, *value.shape)), axes, 0, 0, tiled=True)


def along_z(block):
    return [block] + [lax.ppermute(block, ("z2", "z1"), swap(4, k)) for k in (1, 2, 3)]


def gather_chips(blocks):
    return lax.all_gather(blocks, ("x", "core"), axis=0)


def shards(tokens, keys, values, cotangent, query_weight):
    tok = tokens.T
    feats, count = tok.shape
    cols = keys.shape[1]
    model_width = feats * 16
    scale = 1.0 / math.sqrt(count * 32)
    radius = 0.3 * math.sqrt(model_width + cols * 16)
    whole, half = (8, 2, 2, ROWS, cols), (16, ROWS, cols)
    normt_like = (2, 4, 2, 2, ROWS, count)
    sides = jnp.stack([keys, values, cotangent])

    other = lax.ppermute(tok, "zh", swap(2, 1))
    weight_z = along_z(query_weight)
    *weight_z, other = lax.optimization_barrier((*weight_z, other))
    weight_z = jnp.stack(weight_z)
    weight = gather_chips(weight_z)
    blocks = gather_tokens(jnp.concatenate([tok, other], 0))

    normt, normed, query, keep, send = call(
        lambda *refs: first_kernel(scale, *refs),
        [(normt_like, BF16), ((count, model_width), BF16), ((count, cols), F32), (half, BF16), (half, BF16)],
        48,
        anywhere=(8, 9),
        scratch=(pltpu.VMEM(whole, BF16), pltpu.VMEM(sides.shape, BF16), pltpu.SemaphoreType.DMA((5,))),
    )(*blocks, weight, sides)

    pair = (2 * ROWS, cols)
    partial = call(sum_kernel, [(pair, BF16)], 48)(scatter_parts(keep, send))[0]
    mine = add(partial, lax.ppermute(partial, "z2", swap(2, 1)))
    theirs = lax.ppermute(mine, "z1", swap(2, 1))
    first, square = call(pair_kernel, [((2, *pair), BF16), ((8, HEAD), F32)], 48)(mine, theirs)
    first_all = gather_chips(first)
    square = jnp.sum(everywhere(square, ("zh", "y"), 16), 0)
    square = everywhere(square, ("x", "core"), 8)
    keep, send = call(
        lambda *refs: second_kernel(scale, radius, *refs),
        [(half, BF16), (half, BF16)],
        48,
        anywhere=(4,),
        scratch=(pltpu.VMEM(normt_like, BF16), pltpu.SemaphoreType.DMA((1,))),
    )(square, query, first_all, normed, normt, sides)
    parts = scatter_parts(keep, send).reshape(8, 2, ROWS, cols)
    own, give = call(half_sums_kernel, [((ROWS, cols), F32), ((ROWS, cols), BF16)], 48)(parts)
    return own + lax.ppermute(give, "z2", swap(2, 1)).astype(F32)


def solution(mesh):
    cut = Mesh(mesh.devices.reshape(SIZES), AXES)
    spec = P(AXES[:4], AXES[4:])
    return jax.shard_map(shards, mesh=cut, in_specs=(spec,) * 5, out_specs=spec, check_vma=False)
```

```python
import math

import jax
import jax.numpy as jnp
from jax import lax
from jax.experimental import pallas as pl
from jax.experimental.pallas import tpu as pltpu
from jax.sharding import Mesh, PartitionSpec as P

HEAD = 128
ROWS = 96
EPS = 1e-06
F32 = jnp.float32
BF16 = jnp.bfloat16
AXES = ("z2", "z1", "x", "core", "y", "zh")
SIZES = (2, 2, 4, 2, 8, 2)
STEPS = (0, -1, 1, -2, 2, -3, 3, 4)


def mm(a, b, dims=((1,), (0,))):
    return lax.dot_general(a, b, (dims, ((), ())), preferred_element_type=F32)


def query_grad(query, keys, values, cotangent):
    temper = 1.0 / math.sqrt(HEAD)
    heads = []
    for h in range(query.shape[1] // HEAD):
        cols = slice(h * HEAD, (h + 1) * HEAD)
        q = query[:, cols]
        key, value, cot = keys[:, cols], values[:, cols], cotangent[:, cols]
        center = q - jnp.mean(q, -1, keepdims=True)
        inverse = lax.rsqrt(jnp.mean(center * center, -1, keepdims=True) + EPS)
        qn = center * inverse
        scores = mm(qn.astype(BF16), key, ((1,), (1,))) * temper
        expon = jnp.exp(scores)
        attend = expon / jnp.sum(expon, -1, keepdims=True)
        dprob = mm(cot, value, ((1,), (1,)))
        dscore = attend * (dprob - jnp.sum(attend * dprob, -1, keepdims=True))
        dqn = mm(dscore.astype(BF16), key) * temper
        dq = inverse * (
            dqn
            - jnp.mean(dqn, -1, keepdims=True)
            - qn * jnp.mean(dqn * qn, -1, keepdims=True)
        )
        heads.append(dq.astype(BF16))
    return jnp.concatenate(heads, axis=1)


def fetch(pairs, sems):
    copies = [pltpu.make_async_copy(src, dst, sems.at[i]) for i, (src, dst) in enumerate(pairs)]
    for copy in copies:
        copy.start()
    return copies


def wait(copies):
    for copy in copies:
        copy.wait()


def by_z(src_ref, dst_ref):
    z1, z2 = lax.axis_index("z1"), lax.axis_index("z2")
    return [
        (src_ref.at[:, k], dst_ref.at[:, jnp.bitwise_xor(z1, k % 2), jnp.bitwise_xor(z2, k // 2)]) for k in range(4)
    ]


def first_kernel(scale, *refs):
    toks, refs = refs[:8], refs[8:]
    w_any, sides_any, normt_ref, normed_ref, query_ref, keep_ref, send_ref, w_ref, sides_ref, sems = refs
    copies = fetch(by_z(w_any, w_ref) + [(sides_any, sides_ref)], sems)
    y, zh = lax.axis_index("y"), lax.axis_index("zh")
    width = normed_ref.shape[1]
    total = jnp.zeros((1, normt_ref.shape[-1]), F32)
    for ref in toks:
        total += jnp.sum(ref[...].astype(F32), 0, keepdims=True)
    mean = total / width
    total = jnp.zeros_like(total)
    for ref in toks:
        center = ref[...].astype(F32) - mean
        total += jnp.sum(center * center, 0, keepdims=True)
    inverse = lax.rsqrt(total / width + EPS)
    for ref, step in zip(toks, STEPS):
        block = ((ref[...].astype(F32) - mean) * inverse).astype(BF16)
        from_y = lax.rem(y + (step + 8), 8)
        for part in range(4):
            x = 2 * lax.rem(from_y, 2) + jnp.bitwise_xor(zh, part // 2)
            normt_ref[part % 2, x, lax.rem(from_y // 2, 2), from_y // 4] = block[part * ROWS:(part + 1) * ROWS]
    run = 4 * ROWS
    for x in range(4):
        for c in range(2):
            at = (2 * x + c) * run
            normed_ref[:, at:at + run] = normt_ref[c, x].reshape(run, normt_ref.shape[-1]).T
    wait(copies)
    query = mm(normed_ref[...], w_ref[...].reshape(width, w_ref.shape[-1]))
    query_ref[...] = query
    dq = query_grad(query, sides_ref[0], sides_ref[1], sides_ref[2])
    term(scale, normt_ref, dq, keep_ref, send_ref)


def term(scale, normt_ref, dq, keep_ref, send_ref):
    core = lax.axis_index("core")
    for c, ref in ((core, keep_ref), (1 - core, send_ref)):
        rows = normt_ref[c].reshape(16 * ROWS, normt_ref.shape[-1])
        ref[...] = (mm(rows, dq) * scale).astype(BF16).reshape(ref.shape)


def sum_kernel(parts_ref, out_ref):
    out_ref[...] = jnp.sum(parts_ref[...].astype(F32), 0).astype(BF16)


def half_sums_kernel(parts_ref, own_ref, give_ref):
    z2 = lax.axis_index("z2")
    own_ref[...] = jnp.sum(parts_ref[:, z2].astype(F32), 0)
    give_ref[...] = jnp.sum(parts_ref[:, 1 - z2].astype(F32), 0).astype(BF16)


def pair_kernel(mine_ref, theirs_ref, mine_far_ref, theirs_far_ref, first_ref, square_ref):
    z1 = lax.axis_index("z1")
    mine = mine_ref[...].astype(F32) + mine_far_ref[...].astype(F32)
    theirs = theirs_ref[...].astype(F32) + theirs_far_ref[...].astype(F32)
    first_ref[z1] = mine.astype(BF16)
    first_ref[1 - z1] = theirs.astype(BF16)
    square = jnp.sum((mine * mine + theirs * theirs).reshape(-1, 8, mine.shape[1]), 0)
    square_ref[...] = square[:, :HEAD] + square[:, HEAD:]


def second_kernel(scale, radius, square_ref, query_ref, first_ref, normed_ref, normt_any, sides_ref,
                  keep_ref, send_ref, normt_ref, sems):
    copies = fetch([(normt_any, normt_ref)], sems)
    norm = jnp.sqrt(jnp.sum(jnp.sum(square_ref[...], 0), keepdims=True))
    move = mm(normed_ref[...], first_ref[...].reshape(normed_ref.shape[1], first_ref.shape[-1]))
    query = query_ref[...] + (radius / norm) * move
    dq = query_grad(query, sides_ref[0], sides_ref[1], sides_ref[2])
    wait(copies)
    term(scale, normt_ref, dq, keep_ref, send_ref)


def call(kernel, outs, limit, anywhere=(), scratch=()):
    spec = pl.BlockSpec(memory_space=pltpu.VMEM)

    def run(*args):
        return pl.pallas_call(
            kernel,
            out_shape=[jax.ShapeDtypeStruct(s, d) for s, d in outs],
            in_specs=[pl.BlockSpec(memory_space=pl.ANY) if i in anywhere else spec for i in range(len(args))],
            out_specs=[spec] * len(outs),
            scratch_shapes=list(scratch),
            compiler_params=pltpu.CompilerParams(vmem_limit_bytes=limit * 1024 * 1024),
        )(*args)

    return run


def swap(size, step):
    return [(i, i ^ step) for i in range(size)]


def turn(value, step):
    return lax.ppermute(value, "y", [(i, (i + step) % 8) for i in range(8)])


def after(value, *others):
    return lax.optimization_barrier((value, *others))[0]


def gather_tokens(block):
    back1, ahead1, back2, ahead2 = turn(block, 1), turn(block, 7), turn(block, 2), turn(block, 6)
    back3, ahead3, ahead4 = turn(back2, 1), turn(ahead2, 7), turn(ahead2, 6)
    return block, back1, ahead1, back2, ahead2, back3, ahead3, ahead4


def add(a, b):
    return (a.astype(F32) + b.astype(F32)).astype(BF16)


def scatter_parts(keep, send):
    both = add(keep, lax.ppermute(send, "core", swap(2, 1)))
    pieces = both.reshape(8, 2 * ROWS, both.shape[-1])
    return lax.all_to_all(pieces, ("x", "z1"), 0, 0, tiled=True)


def everywhere(value, axes, size):
    return lax.all_to_all(jnp.broadcast_to(value, (size, *value.shape)), axes, 0, 0, tiled=True)


def along_z(block):
    return [block] + [lax.ppermute(block, ("z2", "z1"), swap(4, k)) for k in (1, 2, 3)]


def gather_chips(blocks):
    return lax.all_gather(blocks, ("x", "core"), axis=0)


def shards(tokens, keys, values, cotangent, query_weight):
    tok = tokens.T
    feats, count = tok.shape
    cols = keys.shape[1]
    model_width = feats * 16
    scale = 1.0 / math.sqrt(count * 32)
    radius = 0.3 * math.sqrt(model_width + cols * 16)
    whole, half = (8, 2, 2, ROWS, cols), (16, ROWS, cols)
    normt_like = (2, 4, 2, 2, ROWS, count)
    sides = jnp.stack([keys, values, cotangent])

    other = lax.ppermute(tok, "zh", swap(2, 1))
    weight_z = along_z(query_weight)
    *weight_z, block = lax.optimization_barrier((*weight_z, jnp.concatenate([tok, other], 0)))
    weight_z = jnp.stack(weight_z)
    weight = gather_chips(weight_z)
    blocks = gather_tokens(block)

    normt, normed, query, keep, send = call(
        lambda *refs: first_kernel(scale, *refs),
        [(normt_like, BF16), ((count, model_width), BF16), ((count, cols), F32), (half, BF16), (half, BF16)],
        48,
        anywhere=(8, 9),
        scratch=(pltpu.VMEM(whole, BF16), pltpu.VMEM(sides.shape, BF16), pltpu.SemaphoreType.DMA((5,))),
    )(*blocks, weight, sides)

    pair = (2 * ROWS, cols)
    partial = call(sum_kernel, [(pair, BF16)], 48)(scatter_parts(keep, send))[0]
    first, square = call(pair_kernel, [((2, *pair), BF16), ((8, HEAD), F32)], 48)(*along_z(partial))
    first_all = gather_chips(first)
    square = jnp.sum(everywhere(square, ("zh", "y"), 16), 0)
    square = everywhere(square, ("x", "core"), 8)
    keep, send = call(
        lambda *refs: second_kernel(scale, radius, *refs),
        [(half, BF16), (half, BF16)],
        48,
        anywhere=(4,),
        scratch=(pltpu.VMEM(normt_like, BF16), pltpu.SemaphoreType.DMA((1,))),
    )(square, query, first_all, normed, normt, sides)
    parts = scatter_parts(keep, send).reshape(8, 2, ROWS, cols)
    own, give = call(half_sums_kernel, [((ROWS, cols), F32), ((ROWS, cols), BF16)], 48)(parts)
    return own + lax.ppermute(give, "z2", swap(2, 1)).astype(F32)


def solution(mesh):
    cut = Mesh(mesh.devices.reshape(SIZES), AXES)
    spec = P(AXES[:4], AXES[4:])
    return jax.shard_map(shards, mesh=cut, in_specs=(spec,) * 5, out_specs=spec, check_vma=False)
```

```python
import math

import jax
import jax.numpy as jnp
from jax import lax
from jax.experimental import pallas as pl
from jax.experimental.pallas import tpu as pltpu
from jax.sharding import Mesh, PartitionSpec as P

HEAD = 128
ROWS = 96
EPS = 1e-06
F32 = jnp.float32
BF16 = jnp.bfloat16
AXES = ("z2", "z1", "x", "core", "y", "zh")
SIZES = (2, 2, 4, 2, 8, 2)
STEPS = (0, -1, 1, -2, 2, -3, 3, 4)


def mm(a, b, dims=((1,), (0,))):
    return lax.dot_general(a, b, (dims, ((), ())), preferred_element_type=F32)


def query_grad(query, keys, values, cotangent):
    temper = 1.0 / math.sqrt(HEAD)
    heads = []
    for h in range(query.shape[1] // HEAD):
        cols = slice(h * HEAD, (h + 1) * HEAD)
        q = query[:, cols]
        key, value, cot = keys[:, cols], values[:, cols], cotangent[:, cols]
        center = q - jnp.mean(q, -1, keepdims=True)
        inverse = lax.rsqrt(jnp.mean(center * center, -1, keepdims=True) + EPS)
        qn = center * inverse
        scores = mm(qn.astype(BF16), key, ((1,), (1,))) * temper
        expon = jnp.exp(scores)
        attend = expon / jnp.sum(expon, -1, keepdims=True)
        dprob = mm(cot, value, ((1,), (1,)))
        dscore = attend * (dprob - jnp.sum(attend * dprob, -1, keepdims=True))
        dqn = mm(dscore.astype(BF16), key) * temper
        dq = inverse * (
            dqn
            - jnp.mean(dqn, -1, keepdims=True)
            - qn * jnp.mean(dqn * qn, -1, keepdims=True)
        )
        heads.append(dq.astype(BF16))
    return jnp.concatenate(heads, axis=1)


def fetch(pairs, sems, first=0):
    copies = [pltpu.make_async_copy(src, dst, sems.at[first + i]) for i, (src, dst) in enumerate(pairs)]
    for copy in copies:
        copy.start()
    return copies


def wait(copies):
    for copy in copies:
        copy.wait()


def by_z(src_ref, dst_ref):
    z1, z2 = lax.axis_index("z1"), lax.axis_index("z2")
    return [
        (src_ref.at[:, k], dst_ref.at[:, jnp.bitwise_xor(z1, k % 2), jnp.bitwise_xor(z2, k // 2)]) for k in range(4)
    ]


def first_kernel(scale, *refs):
    toks, refs = refs[:8], refs[8:]
    w_any, sides_any, normt_ref, normed_ref, query_ref, keep_ref, send_ref, w_ref, sides_ref, sems = refs
    copies = fetch(by_z(w_any, w_ref) + [(sides_any, sides_ref)], sems)
    y, zh = lax.axis_index("y"), lax.axis_index("zh")
    width = normed_ref.shape[1]
    total = jnp.zeros((1, normt_ref.shape[-1]), F32)
    for ref in toks:
        total += jnp.sum(ref[...].astype(F32), 0, keepdims=True)
    mean = total / width
    total = jnp.zeros_like(total)
    for ref in toks:
        center = ref[...].astype(F32) - mean
        total += jnp.sum(center * center, 0, keepdims=True)
    inverse = lax.rsqrt(total / width + EPS)
    for ref, step in zip(toks, STEPS):
        block = ((ref[...].astype(F32) - mean) * inverse).astype(BF16)
        from_y = lax.rem(y + (step + 8), 8)
        for part in range(4):
            x = 2 * lax.rem(from_y, 2) + jnp.bitwise_xor(zh, part // 2)
            normt_ref[part % 2, x, lax.rem(from_y // 2, 2), from_y // 4] = block[part * ROWS:(part + 1) * ROWS]
    run = 4 * ROWS
    for x in range(4):
        for c in range(2):
            at = (2 * x + c) * run
            normed_ref[:, at:at + run] = normt_ref[c, x].reshape(run, normt_ref.shape[-1]).T
    wait(copies)
    query = mm(normed_ref[...], w_ref[...].reshape(width, w_ref.shape[-1]))
    query_ref[...] = query
    dq = query_grad(query, sides_ref[0], sides_ref[1], sides_ref[2])
    term(scale, normt_ref, dq, keep_ref, send_ref)


def term(scale, normt_ref, dq, keep_ref, send_ref):
    core = lax.axis_index("core")
    for c, ref in ((core, keep_ref), (1 - core, send_ref)):
        rows = normt_ref[c].reshape(16 * ROWS, normt_ref.shape[-1])
        ref[...] = (mm(rows, dq) * scale).astype(BF16).reshape(ref.shape)


def sum_kernel(parts_ref, out_ref):
    out_ref[...] = jnp.sum(parts_ref[...].astype(F32), 0).astype(BF16)


def half_sums_kernel(parts_ref, own_ref, give_ref):
    z2 = lax.axis_index("z2")
    own_ref[...] = jnp.sum(parts_ref[:, z2].astype(F32), 0)
    give_ref[...] = jnp.sum(parts_ref[:, 1 - z2].astype(F32), 0).astype(BF16)


def pair_kernel(mine_ref, theirs_ref, mine_far_ref, theirs_far_ref, first_ref, square_ref):
    z1 = lax.axis_index("z1")
    mine = mine_ref[...].astype(F32) + mine_far_ref[...].astype(F32)
    theirs = theirs_ref[...].astype(F32) + theirs_far_ref[...].astype(F32)
    first_ref[z1] = mine.astype(BF16)
    first_ref[1 - z1] = theirs.astype(BF16)
    square = jnp.sum((mine * mine + theirs * theirs).reshape(-1, 8, mine.shape[1]), 0)
    square_ref[...] = square[:, :HEAD] + square[:, HEAD:]


def second_kernel(scale, radius, square_any, query_any, first_any, normed_any, normt_any, sides_any,
                  keep_ref, send_ref, square_ref, query_ref, first_ref, normed_ref, normt_ref, sides_ref, sems):
    cuts = 4
    chips, run = first_ref.shape[0] // cuts, normed_ref.shape[1] // cuts
    pairs = []
    for i in range(cuts):
        rows, cols = pl.ds(i * chips, chips), pl.ds(i * run, run)
        pairs += [(first_any.at[rows], first_ref.at[rows]), (normed_any.at[:, cols], normed_ref.at[:, cols])]
    pairs += [(square_any, square_ref), (query_any, query_ref), (sides_any, sides_ref)]
    copies = fetch(pairs, sems)
    move = jnp.zeros(query_ref.shape, F32)
    for i in range(cuts):
        wait(copies[2 * i:2 * i + 2])
        rows = first_ref[i * chips:(i + 1) * chips].reshape(run, first_ref.shape[-1])
        move += mm(normed_ref[:, i * run:(i + 1) * run], rows)
    late = fetch([(normt_any, normt_ref)], sems, len(copies))
    wait(copies[2 * cuts:])
    norm = jnp.sqrt(jnp.sum(jnp.sum(square_ref[...], 0), keepdims=True))
    query = query_ref[...] + (radius / norm) * move
    dq = query_grad(query, sides_ref[0], sides_ref[1], sides_ref[2])
    wait(late)
    term(scale, normt_ref, dq, keep_ref, send_ref)


def call(kernel, outs, limit, anywhere=(), scratch=()):
    spec = pl.BlockSpec(memory_space=pltpu.VMEM)

    def run(*args):
        return pl.pallas_call(
            kernel,
            out_shape=[jax.ShapeDtypeStruct(s, d) for s, d in outs],
            in_specs=[pl.BlockSpec(memory_space=pl.ANY) if i in anywhere else spec for i in range(len(args))],
            out_specs=[spec] * len(outs),
            scratch_shapes=list(scratch),
            compiler_params=pltpu.CompilerParams(vmem_limit_bytes=limit * 1024 * 1024),
        )(*args)

    return run


def swap(size, step):
    return [(i, i ^ step) for i in range(size)]


def turn(value, step):
    return lax.ppermute(value, "y", [(i, (i + step) % 8) for i in range(8)])


def after(value, *others):
    return lax.optimization_barrier((value, *others))[0]


def gather_tokens(block):
    back1, ahead1, back2, ahead2 = turn(block, 1), turn(block, 7), turn(block, 2), turn(block, 6)
    back3, ahead3, ahead4 = turn(back2, 1), turn(ahead2, 7), turn(ahead2, 6)
    return block, back1, ahead1, back2, ahead2, back3, ahead3, ahead4


def add(a, b):
    return (a.astype(F32) + b.astype(F32)).astype(BF16)


def scatter_parts(keep, send):
    both = add(keep, lax.ppermute(send, "core", swap(2, 1)))
    pieces = both.reshape(8, 2 * ROWS, both.shape[-1])
    return lax.all_to_all(pieces, ("x", "z1"), 0, 0, tiled=True)


def everywhere(value, axes, size):
    return lax.all_to_all(jnp.broadcast_to(value, (size, *value.shape)), axes, 0, 0, tiled=True)


def along_z(block):
    return [block] + [lax.ppermute(block, ("z2", "z1"), swap(4, k)) for k in (1, 2, 3)]


def gather_chips(blocks):
    return lax.all_gather(blocks, ("x", "core"), axis=0)


def shards(tokens, keys, values, cotangent, query_weight):
    tok = tokens.T
    feats, count = tok.shape
    cols = keys.shape[1]
    model_width = feats * 16
    scale = 1.0 / math.sqrt(count * 32)
    radius = 0.3 * math.sqrt(model_width + cols * 16)
    whole, half = (8, 2, 2, ROWS, cols), (16, ROWS, cols)
    normt_like = (2, 4, 2, 2, ROWS, count)
    sides = jnp.stack([keys, values, cotangent])

    other = lax.ppermute(tok, "zh", swap(2, 1))
    weight_z = along_z(query_weight)
    *weight_z, block = lax.optimization_barrier((*weight_z, jnp.concatenate([tok, other], 0)))
    weight_z = jnp.stack(weight_z)
    weight = gather_chips(weight_z)
    blocks = gather_tokens(block)

    normt, normed, query, keep, send = call(
        lambda *refs: first_kernel(scale, *refs),
        [(normt_like, BF16), ((count, model_width), BF16), ((count, cols), F32), (half, BF16), (half, BF16)],
        48,
        anywhere=(8, 9),
        scratch=(pltpu.VMEM(whole, BF16), pltpu.VMEM(sides.shape, BF16), pltpu.SemaphoreType.DMA((5,))),
    )(*blocks, weight, sides)

    pair = (2 * ROWS, cols)
    partial = call(sum_kernel, [(pair, BF16)], 48)(scatter_parts(keep, send))[0]
    first, square = call(pair_kernel, [((2, *pair), BF16), ((8, HEAD), F32)], 48)(*along_z(partial))
    first_all = gather_chips(first)
    square = jnp.sum(everywhere(square, ("zh", "y"), 16), 0)
    square = everywhere(square, ("x", "core"), 8)
    args = (square, query, first_all, normed, normt, sides)
    keep, send = call(
        lambda *refs: second_kernel(scale, radius, *refs),
        [(half, BF16), (half, BF16)],
        51,
        anywhere=range(len(args)),
        scratch=[pltpu.VMEM(arg.shape, arg.dtype) for arg in args] + [pltpu.SemaphoreType.DMA((12,))],
    )(*args)
    parts = scatter_parts(keep, send).reshape(8, 2, ROWS, cols)
    own, give = call(half_sums_kernel, [((ROWS, cols), F32), ((ROWS, cols), BF16)], 48)(parts)
    return own + lax.ppermute(give, "z2", swap(2, 1)).astype(F32)


def solution(mesh):
    cut = Mesh(mesh.devices.reshape(SIZES), AXES)
    spec = P(AXES[:4], AXES[4:])
    return jax.shard_map(shards, mesh=cut, in_specs=(spec,) * 5, out_specs=spec, check_vma=False)
```

```python
import math

import jax
import jax.numpy as jnp
from jax import lax
from jax.experimental import pallas as pl
from jax.experimental.pallas import tpu as pltpu
from jax.sharding import Mesh, PartitionSpec as P

HEAD = 128
ROWS = 96
EPS = 1e-06
F32 = jnp.float32
BF16 = jnp.bfloat16
AXES = ("z2", "z1", "x", "core", "y", "zh")
SIZES = (2, 2, 4, 2, 8, 2)
STEPS = (0, -1, 1, -2, 2, -3, 3, 4)


def mm(a, b, dims=((1,), (0,))):
    return lax.dot_general(a, b, (dims, ((), ())), preferred_element_type=F32)


def query_grad(query, keys, values, cotangent):
    temper = 1.0 / math.sqrt(HEAD)
    heads = []
    for h in range(query.shape[1] // HEAD):
        cols = slice(h * HEAD, (h + 1) * HEAD)
        q = query[:, cols]
        key, value, cot = keys[:, cols], values[:, cols], cotangent[:, cols]
        center = q - jnp.mean(q, -1, keepdims=True)
        inverse = lax.rsqrt(jnp.mean(center * center, -1, keepdims=True) + EPS)
        qn = center * inverse
        scores = mm(qn.astype(BF16), key, ((1,), (1,))) * temper
        expon = jnp.exp(scores)
        attend = expon / jnp.sum(expon, -1, keepdims=True)
        dprob = mm(cot, value, ((1,), (1,)))
        dscore = attend * (dprob - jnp.sum(attend * dprob, -1, keepdims=True))
        dqn = mm(dscore.astype(BF16), key) * temper
        dq = inverse * (
            dqn
            - jnp.mean(dqn, -1, keepdims=True)
            - qn * jnp.mean(dqn * qn, -1, keepdims=True)
        )
        heads.append(dq.astype(BF16))
    return jnp.concatenate(heads, axis=1)


def by_head(array):
    return [array[:, h * HEAD:(h + 1) * HEAD] for h in range(array.shape[1] // HEAD)]


def prob_grads(sides_ref):
    return [mm(cot, value, ((1,), (1,))) for cot, value in zip(by_head(sides_ref[2]), by_head(sides_ref[1]))]


def query_grad_beside(query, keys, dprobs):
    temper = 1.0 / math.sqrt(HEAD)
    keys = by_head(keys)
    centers = [q - jnp.mean(q, -1, keepdims=True) for q in by_head(query)]
    inverses = [lax.rsqrt(jnp.mean(center * center, -1, keepdims=True) + EPS) for center in centers]
    qns = [center * inverse for center, inverse in zip(centers, inverses)]
    scores = [mm(qn.astype(BF16), key, ((1,), (1,))) * temper for qn, key in zip(qns, keys)]
    expons = [jnp.exp(score) for score in scores]
    attends = [expon * (1.0 / jnp.sum(expon, -1, keepdims=True)) for expon in expons]
    means = [jnp.sum(attend * dprob, -1, keepdims=True) for attend, dprob in zip(attends, dprobs)]
    dscores = [attend * (dprob - mean) for attend, dprob, mean in zip(attends, dprobs, means)]
    dqns = [mm(dscore.astype(BF16), key) * temper for dscore, key in zip(dscores, keys)]
    dqs = [
        inverse * (dqn - jnp.mean(dqn, -1, keepdims=True) - qn * jnp.mean(dqn * qn, -1, keepdims=True))
        for inverse, dqn, qn in zip(inverses, dqns, qns)
    ]
    return jnp.concatenate([dq.astype(BF16) for dq in dqs], axis=1)


def fetch(pairs, sems, first=0):
    copies = [pltpu.make_async_copy(src, dst, sems.at[first + i]) for i, (src, dst) in enumerate(pairs)]
    for copy in copies:
        copy.start()
    return copies


def wait(copies):
    for copy in copies:
        copy.wait()


def by_z(src_ref, dst_ref):
    z1, z2 = lax.axis_index("z1"), lax.axis_index("z2")
    return [
        (src_ref.at[:, k], dst_ref.at[:, jnp.bitwise_xor(z1, k % 2), jnp.bitwise_xor(z2, k // 2)]) for k in range(4)
    ]


def first_kernel(scale, *refs):
    toks, refs = refs[:8], refs[8:]
    w_any, sides_any, normt_ref, normed_ref, query_ref, keep_ref, send_ref, w_ref, sides_ref, sems = refs
    copies = fetch(by_z(w_any, w_ref) + [(sides_any, sides_ref)], sems)
    y, zh = lax.axis_index("y"), lax.axis_index("zh")
    width = normed_ref.shape[1]
    total = jnp.zeros((1, normt_ref.shape[-1]), F32)
    for ref in toks:
        total += jnp.sum(ref[...].astype(F32), 0, keepdims=True)
    mean = total / width
    total = jnp.zeros_like(total)
    for ref in toks:
        center = ref[...].astype(F32) - mean
        total += jnp.sum(center * center, 0, keepdims=True)
    inverse = lax.rsqrt(total / width + EPS)
    for ref, step in zip(toks, STEPS):
        block = ((ref[...].astype(F32) - mean) * inverse).astype(BF16)
        from_y = lax.rem(y + (step + 8), 8)
        for part in range(4):
            x = 2 * lax.rem(from_y, 2) + jnp.bitwise_xor(zh, part // 2)
            normt_ref[part % 2, x, lax.rem(from_y // 2, 2), from_y // 4] = block[part * ROWS:(part + 1) * ROWS]
    run = 4 * ROWS
    for x in range(4):
        for c in range(2):
            at = (2 * x + c) * run
            normed_ref[:, at:at + run] = normt_ref[c, x].reshape(run, normt_ref.shape[-1]).T
    wait(copies)
    query = mm(normed_ref[...], w_ref[...].reshape(width, w_ref.shape[-1]))
    query_ref[...] = query
    dq = query_grad(query, sides_ref[0], sides_ref[1], sides_ref[2])
    term(scale, normt_ref, dq, keep_ref, send_ref)


def term(scale, normt_ref, dq, keep_ref, send_ref):
    core = lax.axis_index("core")
    for c, ref in ((core, keep_ref), (1 - core, send_ref)):
        rows = normt_ref[c].reshape(16 * ROWS, normt_ref.shape[-1])
        ref[...] = (mm(rows, dq) * scale).astype(BF16).reshape(ref.shape)


def sum_kernel(parts_ref, out_ref):
    out_ref[...] = jnp.sum(parts_ref[...].astype(F32), 0).astype(BF16)


def half_sums_kernel(parts_ref, own_ref, give_ref):
    z2 = lax.axis_index("z2")
    own_ref[...] = jnp.sum(parts_ref[:, z2].astype(F32), 0)
    give_ref[...] = jnp.sum(parts_ref[:, 1 - z2].astype(F32), 0).astype(BF16)


def pair_kernel(mine_ref, theirs_ref, mine_far_ref, theirs_far_ref, first_ref, square_ref):
    z1 = lax.axis_index("z1")
    mine = mine_ref[...].astype(F32) + mine_far_ref[...].astype(F32)
    theirs = theirs_ref[...].astype(F32) + theirs_far_ref[...].astype(F32)
    first_ref[z1] = mine.astype(BF16)
    first_ref[1 - z1] = theirs.astype(BF16)
    square = jnp.sum((mine * mine + theirs * theirs).reshape(-1, 8, mine.shape[1]), 0)
    square_ref[...] = square[:, :HEAD] + square[:, HEAD:]


def second_kernel(scale, radius, square_any, query_any, first_any, normed_any, normt_any, sides_any,
                  keep_ref, send_ref, square_ref, query_ref, first_ref, normed_ref, normt_ref, sides_ref, sems):
    cuts = 4
    chips, run = first_ref.shape[0] // cuts, normed_ref.shape[1] // cuts
    pairs = [(sides_any, sides_ref)]
    for i in range(cuts):
        rows, cols = pl.ds(i * chips, chips), pl.ds(i * run, run)
        pairs += [(first_any.at[rows], first_ref.at[rows]), (normed_any.at[:, cols], normed_ref.at[:, cols])]
    pairs += [(square_any, square_ref), (query_any, query_ref)]
    copies = fetch(pairs, sems)
    wait(copies[:1])
    dprobs = prob_grads(sides_ref)
    copies = copies[1:]
    move = jnp.zeros(query_ref.shape, F32)
    for i in range(cuts):
        wait(copies[2 * i:2 * i + 2])
        rows = first_ref[i * chips:(i + 1) * chips].reshape(run, first_ref.shape[-1])
        move += mm(normed_ref[:, i * run:(i + 1) * run], rows)
    late = fetch([(normt_any, normt_ref)], sems, len(pairs))
    wait(copies[2 * cuts:])
    norm = jnp.sqrt(jnp.sum(jnp.sum(square_ref[...], 0), keepdims=True))
    query = query_ref[...] + (radius / norm) * move
    dq = query_grad_beside(query, sides_ref[0], dprobs)
    wait(late)
    term(scale, normt_ref, dq, keep_ref, send_ref)


def call(kernel, outs, limit, anywhere=(), scratch=()):
    spec = pl.BlockSpec(memory_space=pltpu.VMEM)

    def run(*args):
        return pl.pallas_call(
            kernel,
            out_shape=[jax.ShapeDtypeStruct(s, d) for s, d in outs],
            in_specs=[pl.BlockSpec(memory_space=pl.ANY) if i in anywhere else spec for i in range(len(args))],
            out_specs=[spec] * len(outs),
            scratch_shapes=list(scratch),
            compiler_params=pltpu.CompilerParams(vmem_limit_bytes=limit * 1024 * 1024),
        )(*args)

    return run


def swap(size, step):
    return [(i, i ^ step) for i in range(size)]


def turn(value, step):
    return lax.ppermute(value, "y", [(i, (i + step) % 8) for i in range(8)])


def after(value, *others):
    return lax.optimization_barrier((value, *others))[0]


def gather_tokens(block):
    back1, ahead1, back2, ahead2 = turn(block, 1), turn(block, 7), turn(block, 2), turn(block, 6)
    back3, ahead3, ahead4 = turn(back2, 1), turn(ahead2, 7), turn(ahead2, 6)
    return block, back1, ahead1, back2, ahead2, back3, ahead3, ahead4


def add(a, b):
    return (a.astype(F32) + b.astype(F32)).astype(BF16)


def scatter_parts(keep, send):
    both = add(keep, lax.ppermute(send, "core", swap(2, 1)))
    pieces = both.reshape(8, 2 * ROWS, both.shape[-1])
    return lax.all_to_all(pieces, ("x", "z1"), 0, 0, tiled=True)


def everywhere(value, axes, size):
    return lax.all_to_all(jnp.broadcast_to(value, (size, *value.shape)), axes, 0, 0, tiled=True)


def along_z(block):
    return [block] + [lax.ppermute(block, ("z2", "z1"), swap(4, k)) for k in (1, 2, 3)]


def gather_chips(blocks):
    return lax.all_gather(blocks, ("x", "core"), axis=0)


def shards(tokens, keys, values, cotangent, query_weight):
    tok = tokens.T
    feats, count = tok.shape
    cols = keys.shape[1]
    model_width = feats * 16
    scale = 1.0 / math.sqrt(count * 32)
    radius = 0.3 * math.sqrt(model_width + cols * 16)
    whole, half = (8, 2, 2, ROWS, cols), (16, ROWS, cols)
    normt_like = (2, 4, 2, 2, ROWS, count)
    sides = jnp.stack([keys, values, cotangent])

    other = lax.ppermute(tok, "zh", swap(2, 1))
    weight_z = along_z(query_weight)
    *weight_z, block = lax.optimization_barrier((*weight_z, jnp.concatenate([tok, other], 0)))
    weight_z = jnp.stack(weight_z)
    weight = gather_chips(weight_z)
    blocks = gather_tokens(block)

    normt, normed, query, keep, send = call(
        lambda *refs: first_kernel(scale, *refs),
        [(normt_like, BF16), ((count, model_width), BF16), ((count, cols), F32), (half, BF16), (half, BF16)],
        48,
        anywhere=(8, 9),
        scratch=(pltpu.VMEM(whole, BF16), pltpu.VMEM(sides.shape, BF16), pltpu.SemaphoreType.DMA((5,))),
    )(*blocks, weight, sides)

    pair = (2 * ROWS, cols)
    partial = call(sum_kernel, [(pair, BF16)], 48)(scatter_parts(keep, send))[0]
    first, square = call(pair_kernel, [((2, *pair), BF16), ((8, HEAD), F32)], 48)(*along_z(partial))
    first_all = gather_chips(first)
    square = jnp.sum(everywhere(square, ("zh", "y"), 16), 0)
    square = everywhere(square, ("x", "core"), 8)
    args = (square, query, first_all, normed, normt, sides)
    keep, send = call(
        lambda *refs: second_kernel(scale, radius, *refs),
        [(half, BF16), (half, BF16)],
        51,
        anywhere=range(len(args)),
        scratch=[pltpu.VMEM(arg.shape, arg.dtype) for arg in args] + [pltpu.SemaphoreType.DMA((12,))],
    )(*args)
    parts = scatter_parts(keep, send).reshape(8, 2, ROWS, cols)
    own, give = call(half_sums_kernel, [((ROWS, cols), F32), ((ROWS, cols), BF16)], 48)(parts)
    return own + lax.ppermute(give, "z2", swap(2, 1)).astype(F32)


def solution(mesh):
    cut = Mesh(mesh.devices.reshape(SIZES), AXES)
    spec = P(AXES[:4], AXES[4:])
    return jax.shard_map(shards, mesh=cut, in_specs=(spec,) * 5, out_specs=spec, check_vma=False)
```
